256 devices in a mesh: dp: 4 (over z_hi, core), ctx: 64 (over y, z_lo, x).
Axes of the slice: x: 4, y: 4, z: 8 (z_hi: 2, z_lo: 4; z = z_hi * 4 + z_lo), core: 2. Of those that a mesh axis runs over, the one named last changes fastest.
Arguments:
- query_in: bfloat16 [4, 8192, 512], P('dp', 'ctx'), may hold values from -6 to 6
- key_in: bfloat16 [4, 8192, 512], P('dp', 'ctx'), may hold values from -6 to 6
- value_in: bfloat16 [4, 8192, 512], P('dp', 'ctx'), may hold values from -6 to 6
- short_taps: float32 [3, 3, 512], replicated, may hold values from -3 to 3
- long_filter: float32 [8192, 512], P('ctx'), may hold values from -6 to 6
- cotangent: bfloat16 [4, 8192, 512], P('dp', 'ctx'), may hold values from -6 to 6
Outputs:
- grad_query: bfloat16 [4, 8192, 512], P('dp', 'ctx')
- grad_key: bfloat16 [4, 8192, 512], P('dp', 'ctx')
- grad_value: bfloat16 [4, 8192, 512], P('dp', 'ctx')
- grad_taps: float32 [3, 3, 512], replicated
- grad_filter: float32 [8192, 512], P('ctx')
The draws below stay inside these ranges and needn't reach their ends.
All inputs are finite; a program needn't handle non-finite values.
Results may differ from the reference program's by a relative error of at most 0.014.
Values may be sent and summed in bfloat16 or wider, within the bound.
A program may use at most 64 MiB of HBM per device.

```python
import math
import jax
import jax.numpy as jnp
from jax import lax

CH = 512
TAPS = 3
SEQ_LEN = 8192
SEQS = 4


def level_of(key, dims, pieces, least, high):
    def one(position, parts):
        heights = jax.random.uniform(jax.random.fold_in(jax.random.fold_in(key, 6), position), (parts,), jnp.float32, least / len(pieces), high / len(pieces))
        return jnp.repeat(jnp.exp(heights), dims[position] // parts).reshape((-1,) + (1,) * (len(dims) - position - 1))

    level = one(*pieces[0])
    for cut in pieces[1:]:
        level = level * one(*cut)
    return level


def bell_draw(key, dims, scale, bound, pieces=(), held_as=jnp.bfloat16):
    factor_of = level_of(key, dims, pieces, -0.22, 0.18) if pieces else 1.0
    drawn = jax.random.normal(key, dims, jnp.float32) * scale * factor_of
    return jnp.minimum(jnp.maximum(drawn, -bound), bound).astype(held_as)


def setup_inputs(seed: int = 0) -> dict:
    seeds = jax.random.split(jax.random.key(seed), 7)
    query_in = bell_draw(seeds[0], (SEQS, SEQ_LEN, CH), 1.0, 6.0, ((0, 4), (1, 64)))
    key_in = bell_draw(seeds[1], (SEQS, SEQ_LEN, CH), 1.0, 6.0, ((0, 4), (1, 64)))
    value_in = bell_draw(seeds[2], (SEQS, SEQ_LEN, CH), 1.0, 6.0, ((0, 4), (1, 64)))
    short_taps = bell_draw(seeds[3], (3, TAPS, CH), 0.6, 3.0, (), jnp.float32)
    long_filter = bell_draw(seeds[4], (SEQ_LEN, CH), 1.0, 6.0, ((0, 64),), jnp.float32)
    cotangent = bell_draw(seeds[5], (SEQS, SEQ_LEN, CH), 1.0, 6.0, ((0, 4), (1, 64)))
    return {"query_in": query_in, "key_in": key_in, "value_in": value_in, "short_taps": short_taps, "long_filter": long_filter, "cotangent": cotangent}


def causal_taps(signal, taps_row):
    padded = jnp.pad(signal, ((TAPS - 1, 0), (0, 0)))
    total = jnp.zeros_like(signal)
    for offset in range(TAPS):
        total = total + taps_row[offset] * padded[TAPS - 1 - offset:TAPS - 1 - offset + SEQ_LEN]
    return (total, padded)

def adjoint_taps(gradient, taps_row):
    padded = jnp.pad(gradient, ((0, TAPS - 1), (0, 0)))
    total = jnp.zeros_like(gradient)
    for offset in range(TAPS):
        total = total + taps_row[offset] * padded[offset:offset + SEQ_LEN]
    return total

def reference(query_in, key_in, value_in, short_taps, long_filter, cotangent):
    norm_factor = 1.0 / math.sqrt(SEQ_LEN)
    padded_length = 2 * SEQ_LEN
    filter_spec = jnp.fft.rfft(long_filter, n=padded_length, axis=0)
    tap_total = jnp.zeros((3, TAPS, CH), jnp.float32)
    filter_total = jnp.zeros((SEQ_LEN, CH), jnp.float32)
    outputs = [[], [], []]
    for sequence in range(SEQS):
        sources = [query_in[sequence].astype(jnp.float32), key_in[sequence].astype(jnp.float32), value_in[sequence].astype(jnp.float32)]
        feats = [causal_taps(sources[branch], short_taps[branch]) for branch in range(3)]
        query_feat, key_feat, value_feat = (feats[0][0], feats[1][0], feats[2][0])
        upstream = cotangent[sequence].astype(jnp.float32)
        mixed_field = key_feat * value_feat
        gated_field = upstream * query_feat
        mix_spec = jnp.fft.rfft(mixed_field, n=padded_length, axis=0)
        grad_spec = jnp.fft.rfft(gated_field, n=padded_length, axis=0)
        convolved = jnp.fft.irfft(filter_spec * mix_spec, n=padded_length, axis=0)[:SEQ_LEN] * norm_factor
        adjoint = jnp.fft.irfft(jnp.conj(filter_spec) * grad_spec, n=padded_length, axis=0)[:SEQ_LEN] * norm_factor
        filter_total = filter_total + jnp.fft.irfft(jnp.conj(mix_spec) * grad_spec, n=padded_length, axis=0)[:SEQ_LEN] * norm_factor
        d_feats = [upstream * convolved, adjoint * value_feat, adjoint * key_feat]
        tap_rows = []
        for branch in range(3):
            outputs[branch].append(adjoint_taps(d_feats[branch], short_taps[branch]))
            padded_in = feats[branch][1]
            tap_rows.append(jnp.stack([lax.optimization_barrier(jnp.sum(d_feats[branch] * padded_in[TAPS - 1 - offset:TAPS - 1 - offset + SEQ_LEN], axis=0)) for offset in range(TAPS)]))
        tap_total = tap_total + jnp.stack(tap_rows)
    grad_taps = tap_total / math.sqrt(SEQS * SEQ_LEN)
    return (jnp.stack(outputs[0]).astype(jnp.bfloat16), jnp.stack(outputs[1]).astype(jnp.bfloat16), jnp.stack(outputs[2]).astype(jnp.bfloat16), grad_taps, filter_total)
```

```python
import functools
import math

import jax
import jax.numpy as jnp
import numpy as np
from jax import lax
from jax.experimental import pallas as pl
from jax.experimental.pallas import tpu as pltpu
from jax.sharding import PartitionSpec as P

MESH = pl.DeviceIdType.MESH
F32 = jnp.float32
BF16 = jnp.bfloat16

NZ, NPLANE, NCTX = 8, 16, 64
GROUP = NZ * NPLANE
CHAN = 4
SEQ = 2
POS = 128
ROWS = 16


def split_np(table):
    high = table.astype(jnp.bfloat16)
    low = (table - high.astype(np.float64)).astype(jnp.bfloat16)
    return high, low


@functools.cache
def tables():
    length = NCTX * POS
    a = np.arange(NCTX, dtype=np.float64)
    b = np.arange(POS, dtype=np.float64)
    outer = 2 * np.pi * np.outer(a, a + 0.25) / NCTX
    turn = 2 * np.pi * np.outer(a + 0.25, b) / length
    inner = 2 * np.pi * (np.outer(b, b) % POS) / POS
    first = np.concatenate([np.cos(outer.T), -np.sin(outer.T)], axis=0)
    high, low = split_np(first)
    first_cat = np.concatenate([high, low, high], axis=1)
    scale = 1.0 / (length * math.sqrt(length))
    last = np.concatenate([np.cos(outer), -np.sin(outer)], axis=1) * scale
    high, low = split_np(last)
    last_cat = np.concatenate([high, low, high], axis=1)
    c, s = np.cos(inner), np.sin(inner)
    forward = np.stack(split_np(np.block([[c, -s], [s, c]])))
    inverse = np.stack(split_np(np.block([[c, s], [-s, c]])))
    twiddle = np.stack([np.cos(turn), np.sin(turn)]).astype(np.float32)
    pick = np.zeros((32, 4, CHAN, 4, POS), np.float32)
    for g in range(32):
        for f in range(4):
            for i in range(CHAN):
                pick[g, f, i, f, CHAN * g + i] = 1
    pick = pick.reshape(512, 512).astype(jnp.bfloat16)
    pick_one = np.zeros((32, 8, POS), np.float32)
    for g in range(32):
        for i in range(CHAN):
            pick_one[g, i, CHAN * g + i] = 1
    pick_one = pick_one.reshape(256, POS).astype(jnp.bfloat16)
    return first_cat, last_cat, forward, inverse, twiddle, pick, pick_one


def split(x):
    high = x.astype(BF16)
    return high, (x - high.astype(F32)).astype(BF16)


def dot(a, b):
    return jnp.dot(a, b, preferred_element_type=F32)


def dot_nt(a, b):
    return lax.dot_general(a, b, (((1,), (1,)), ((), ())), preferred_element_type=F32)


def stack_split(x):
    high, low = split(x)
    return jnp.concatenate([high, high, low], axis=0)


def wide_dot(x, table):
    high, low = split(x)
    return dot(high, table[0]) + (dot(high, table[1]) + dot(low, table[0]))


def kernel(
    q_ref, k_ref, v_ref, c_ref, filt_ref, taps_ref,
    first_ref, last_ref, fwd_ref, inv_ref, tw_ref, pick_ref, pick1_ref,
    gq_ref, gk_ref, gv_ref, gt_ref, gf_ref,
    send_buf, recv_buf, fsend, frecv, raw, fraw, spec, hspec, keep, pack, rsend, rrecv,
    corr_buf, sib_send, sib_recv, tap_rows, tap_own, tap_sib, tap_send, tap_recv,
    send_sem, recv_sem, fsend_sem, frecv_sem, rsend_sem, rrecv_sem,
    sib_sems, tap_sems, plane_sem,
):
    dp, cx = lax.axis_index("dp"), lax.axis_index("ctx")
    zh, core = dp // 2, lax.rem(dp, 2)
    y, zl, x = cx // 16, lax.rem(cx // 4, 4), lax.rem(cx, 4)
    z = zh * 4 + zl
    me = zh * NCTX + cx

    def place(zt, yt, xt, core_t):
        half = zt // 4
        ctx = yt * 16 + lax.rem(zt, 4) * 4 + xt
        return (half * 2 + core_t, ctx), half * NCTX + ctx

    def in_plane(zt, r):
        return place(zt, lax.rem(y + r // 4, 4), lax.rem(x + lax.rem(r, 4), 4), core)

    def plane_of(k):
        return lax.rem(z + k, NZ)

    sibling = (zh * 2 + (1 - core), cx)

    barrier = pltpu.get_barrier_semaphore()

    def greet(r, carry):
        pl.semaphore_signal(barrier, inc=1, device_id=in_plane(z, r)[0], device_id_type=MESH)
        return carry

    lax.fori_loop(1, NPLANE, greet, 0)
    for k in range(1, NZ):
        pl.semaphore_signal(barrier, inc=1, device_id=place(plane_of(k), y, x, core)[0], device_id_type=MESH)
    pl.semaphore_signal(barrier, inc=1, device_id=sibling, device_id_type=MESH)

    for j in range(4):
        lanes = slice(j * POS, (j + 1) * POS)
        fields = jnp.concatenate([q_ref[:, lanes], k_ref[:, lanes], v_ref[:, lanes], c_ref[:, lanes]], axis=1)
        rows = dot_nt(pick_ref[...], fields).astype(BF16)
        send_buf[pl.ds(j * 32, 32)] = rows.reshape(32, ROWS, POS)
        high, low = split(filt_ref[:, lanes])
        rows = dot_nt(pick1_ref[...], high) + dot_nt(pick1_ref[...], low)
        fsend[pl.ds(j * 32, 32)] = rows.reshape(32, 8, POS)[:, :CHAN, :]

    pl.semaphore_wait(barrier, NPLANE - 1 + NZ - 1 + 1)
    for k in range(1, NZ):
        pl.semaphore_signal(
            plane_sem.at[NZ - k], inc=1, device_id=place(plane_of(k), y, x, core)[0], device_id_type=MESH
        )

    near = (0, 1, 2, 7)
    own = pltpu.make_async_copy(send_buf.at[me], recv_buf.at[me], recv_sem.at[zh])
    own.start()
    fown = pltpu.make_async_copy(fsend.at[me], frecv.at[cx], frecv_sem)
    fown.start()
    for k in (0, 7, 1, 6, 2, 5, 3, 4):
        if k:
            pl.semaphore_wait(plane_sem.at[k], 1)

        def send(r, carry, k=k):
            to, owner = in_plane(plane_of(k), r)
            if k in near:
                pltpu.make_async_remote_copy(
                    src_ref=fsend.at[owner], dst_ref=frecv.at[cx], send_sem=fsend_sem, recv_sem=frecv_sem,
                    device_id=to, device_id_type=MESH,
                ).start()
            pltpu.make_async_remote_copy(
                src_ref=send_buf.at[owner], dst_ref=recv_buf.at[me], send_sem=send_sem, recv_sem=recv_sem.at[zh],
                device_id=to, device_id_type=MESH,
            ).start()
            return carry

        lax.fori_loop(0 if k else 1, NPLANE, send, 0)

    def wait_bytes(ref, sem):
        pltpu.make_async_copy(ref, ref, sem).wait()

    row_id = lax.broadcasted_iota(jnp.int32, (NCTX, POS), 0)
    lane_id = lax.broadcasted_iota(jnp.int32, (NCTX, POS), 1)

    def before(v, s):
        turned = pltpu.roll(v, s, 1)
        carried = jnp.where(row_id == 0, 0.0, pltpu.roll(turned, 1, 0))
        return jnp.where(lane_id < s, carried, turned)

    def after(v, s):
        turned = pltpu.roll(v, POS - s, 1)
        carried = jnp.where(row_id == NCTX - 1, 0.0, pltpu.roll(turned, NCTX - 1, 0))
        return jnp.where(lane_id >= POS - s, carried, turned)

    def tap(branch, j, i):
        return taps_ref[branch * 3 + j, me * CHAN + i]

    def field(h, f, i):
        return raw[pl.ds(h * NCTX * ROWS + f * CHAN + i, NCTX, ROWS), :]

    cos, sin = tw_ref[0], tw_ref[1]

    def spectrum(values):
        turned = dot(first_ref[...], stack_split(jnp.concatenate(values, axis=1)))
        parts = []
        for n in range(len(values)):
            re, im = turned[:NCTX, n * POS:(n + 1) * POS], turned[NCTX:, n * POS:(n + 1) * POS]
            parts.append(jnp.concatenate([re * cos + im * sin, im * cos - re * sin], axis=1))
        return wide_dot(jnp.concatenate(parts, axis=0), fwd_ref)

    def signal(spectra):
        joined = jnp.concatenate([jnp.concatenate(s, axis=1) for s in spectra], axis=0)
        turned = wide_dot(joined, inv_ref)
        parts = []
        for n in range(len(spectra)):
            re, im = turned[n * NCTX:(n + 1) * NCTX, :POS], turned[n * NCTX:(n + 1) * NCTX, POS:]
            parts.append(jnp.concatenate([re * cos - im * sin, re * sin + im * cos], axis=0))
        return dot(last_ref[...], stack_split(jnp.concatenate(parts, axis=1)))

    def halves(ref, n):
        return ref[n * NCTX:(n + 1) * NCTX, :POS], ref[n * NCTX:(n + 1) * NCTX, POS:]

    wait_bytes(frecv, frecv_sem)
    filt = frecv[...]
    fraw[...] = jnp.concatenate([filt, jnp.zeros_like(filt)], axis=1).reshape(NCTX * 8, POS)
    hspec[...] = spectrum([fraw[pl.ds(i, NCTX, 8), :] for i in range(CHAN)])

    for h in range(SEQ):
        wait_bytes(recv_buf.at[pl.ds(h * NCTX, NCTX)], recv_sem.at[h])
        raw[pl.ds(h * NCTX * ROWS, NCTX * ROWS), :] = (
            recv_buf[pl.ds(h * NCTX, NCTX)].astype(F32).reshape(NCTX * ROWS, POS)
        )
        values = []
        for i in range(CHAN):
            feats = []
            for branch in range(3):
                v = field(h, branch, i)
                feats.append(
                    tap(branch, 0, i) * v + tap(branch, 1, i) * before(v, 1) + tap(branch, 2, i) * before(v, 2)
                )
            keep[h, i, 0] = feats[1]
            keep[h, i, 1] = feats[2]
            values += [feats[1] * feats[2], feats[0] * field(h, 3, i)]
        spec[h] = spectrum(values)

    corrs = []
    for i in range(CHAN):
        re = im = 0.0
        for h in range(SEQ):
            mr, mi = halves(spec.at[h], 2 * i)
            gr, gi = halves(spec.at[h], 2 * i + 1)
            re, im = re + (mr * gr + mi * gi), im + (mr * gi - mi * gr)
        corrs.append((re, im))
    sib_send[...] = signal(corrs)
    sib = pltpu.make_async_remote_copy(
        src_ref=sib_send, dst_ref=sib_recv, send_sem=sib_sems.at[0], recv_sem=sib_sems.at[1],
        device_id=sibling, device_id_type=MESH,
    )
    sib.start()

    tap_rows[...] = jnp.zeros_like(tap_rows)
    for h in range(SEQ):
        spectra = []
        for i in range(CHAN):
            fr, fi = halves(hspec, i)
            mr, mi = halves(spec.at[h], 2 * i)
            gr, gi = halves(spec.at[h], 2 * i + 1)
            spectra += [(fr * mr - fi * mi, fr * mi + fi * mr), (fr * gr + fi * gi, fr * gi - fi * gr)]
        back = signal(spectra)
        for i in range(CHAN):
            conv = back[:, 2 * i * POS:(2 * i + 1) * POS]
            adj = back[:, (2 * i + 1) * POS:(2 * i + 2) * POS]
            grads = [field(h, 3, i) * conv, adj * keep[h, i, 1], adj * keep[h, i, 0]]
            for branch in range(3):
                d, v = grads[branch], field(h, branch, i)
                pack[pl.ds(h * NCTX * ROWS + branch * CHAN + i, NCTX, ROWS), :] = (
                    tap(branch, 0, i) * d + tap(branch, 1, i) * after(d, 1) + tap(branch, 2, i) * after(d, 2)
                )
                for j in range(3):
                    term = d * (before(v, j) if j else v)
                    row = (branch * 3 + j) * CHAN + i
                    tap_rows[row:row + 1, :] += jnp.sum(term, axis=0, keepdims=True)

    ones = jnp.ones((8, POS), F32)
    scale = 1.0 / math.sqrt(SEQ * 2 * NCTX * POS)
    sums = lax.dot_general(
        ones, tap_rows[...], (((1,), (1,)), ((), ())), precision=lax.Precision.HIGHEST, preferred_element_type=F32
    )
    tap_own[...] = sums[0:1] * scale
    tap_sibling = pltpu.make_async_remote_copy(
        src_ref=tap_own, dst_ref=tap_sib, send_sem=tap_sems.at[0], recv_sem=tap_sems.at[1],
        device_id=sibling, device_id_type=MESH,
    )
    tap_sibling.start()

    sib.wait_recv()
    for i in range(CHAN):
        total = sib_send[:, i * POS:(i + 1) * POS] + sib_recv[:, i * POS:(i + 1) * POS]
        for h in range(SEQ):
            pack[pl.ds(h * NCTX * ROWS + 3 * CHAN + i, NCTX, ROWS), :] = total
    rsend[...] = pack[...].reshape(GROUP, ROWS, POS).astype(BF16)

    rown = pltpu.make_async_copy(rsend.at[me], rrecv.at[me], rrecv_sem)
    rown.start()
    for k in (0, 7, 1, 6, 2, 5, 3, 4):
        def give(r, carry, k=k):
            to, owner = in_plane(plane_of(k), r)
            pltpu.make_async_remote_copy(
                src_ref=rsend.at[owner], dst_ref=rrecv.at[me], send_sem=rsend_sem, recv_sem=rrecv_sem,
                device_id=to, device_id_type=MESH,
            ).start()
            return carry

        lax.fori_loop(0 if k else 1, NPLANE, give, 0)

    tap_sibling.wait_recv()
    tap_send[...] = tap_own[...] + tap_sib[...]
    town = pltpu.make_async_copy(tap_send, tap_recv.at[me], tap_sems.at[3])
    town.start()
    for k in (0, 7, 1, 6, 2, 5, 3, 4):
        def tell(r, carry, k=k):
            to, owner = in_plane(plane_of(k), r)
            pltpu.make_async_remote_copy(
                src_ref=tap_send, dst_ref=tap_recv.at[me], send_sem=tap_sems.at[2], recv_sem=tap_sems.at[3],
                device_id=to, device_id_type=MESH,
            ).start()
            return carry

        lax.fori_loop(0 if k else 1, NPLANE, tell, 0)

    wait_bytes(send_buf.at[pl.ds(0, GROUP - 1)], send_sem)
    wait_bytes(fsend.at[pl.ds(0, NCTX - 1)], fsend_sem)
    sib.wait_send()
    tap_sibling.wait_send()

    wait_bytes(tap_recv, tap_sems.at[3])
    taps_all = tap_recv[...].reshape(GROUP, POS)
    total = jnp.zeros((16, GROUP * CHAN), F32)
    for i in range(CHAN):
        pick_row = (
            lax.broadcasted_iota(jnp.int32, (16, POS), 1)
            == CHAN * lax.broadcasted_iota(jnp.int32, (16, POS), 0) + i
        ).astype(F32)
        spread = (
            lax.broadcasted_iota(jnp.int32, (GROUP, GROUP * CHAN), 1)
            == CHAN * lax.broadcasted_iota(jnp.int32, (GROUP, GROUP * CHAN), 0) + i
        ).astype(F32)
        rows = lax.dot_general(
            pick_row, taps_all, (((1,), (1,)), ((), ())),
            precision=lax.Precision.HIGHEST, preferred_element_type=F32,
        )
        total += jnp.dot(rows, spread, precision=lax.Precision.HIGHEST, preferred_element_type=F32)
    gt_ref[...] = total

    wait_bytes(rrecv, rrecv_sem)
    for j in range(4):
        lanes = slice(j * POS, (j + 1) * POS)
        rows = rrecv[pl.ds(j * 32, 32)].reshape(512, POS)
        out = lax.dot_general(rows, pick_ref[...], (((0,), (0,)), ((), ())), preferred_element_type=F32)
        gq_ref[:, lanes] = out[:, :POS].astype(BF16)
        gk_ref[:, lanes] = out[:, POS:2 * POS].astype(BF16)
        gv_ref[:, lanes] = out[:, 2 * POS:3 * POS].astype(BF16)
        gf_ref[:, lanes] = out[:, 3 * POS:]
    wait_bytes(rsend.at[pl.ds(0, GROUP - 1)], rsend_sem)
    for _ in range(1):
        wait_bytes(tap_recv.at[pl.ds(0, GROUP - 1)], tap_sems.at[2])


def per_device(query_in, key_in, value_in, short_taps, long_filter, cotangent):
    rows, channels = query_in.shape[1:]
    vmem = pl.BlockSpec(memory_space=pltpu.VMEM)
    shape = jax.ShapeDtypeStruct
    scratch = [
        pltpu.VMEM((GROUP, ROWS, POS), BF16),
        pltpu.VMEM((GROUP, ROWS, POS), BF16),
        pltpu.VMEM((GROUP, CHAN, POS), F32),
        pltpu.VMEM((NCTX, CHAN, POS), F32),
        pltpu.VMEM((GROUP * ROWS, POS), F32),
        pltpu.VMEM((NCTX * 8, POS), F32),
        pltpu.VMEM((SEQ, 2 * CHAN * NCTX, 2 * POS), F32),
        pltpu.VMEM((CHAN * NCTX, 2 * POS), F32),
        pltpu.VMEM((SEQ, CHAN, 2, NCTX, POS), F32),
        pltpu.VMEM((GROUP * ROWS, POS), F32),
        pltpu.VMEM((GROUP, ROWS, POS), BF16),
        pltpu.VMEM((GROUP, ROWS, POS), BF16),
        pltpu.VMEM((8, POS), F32),
        pltpu.VMEM((NCTX, CHAN * POS), F32),
        pltpu.VMEM((NCTX, CHAN * POS), F32),
        pltpu.VMEM((POS, POS), F32),
        pltpu.VMEM((1, POS), F32),
        pltpu.VMEM((1, POS), F32),
        pltpu.VMEM((1, POS), F32),
        pltpu.VMEM((GROUP, 1, POS), F32),
        pltpu.SemaphoreType.DMA,
        pltpu.SemaphoreType.DMA((SEQ,)),
        pltpu.SemaphoreType.DMA,
        pltpu.SemaphoreType.DMA,
        pltpu.SemaphoreType.DMA,
        pltpu.SemaphoreType.DMA,
        pltpu.SemaphoreType.DMA((2,)),
        pltpu.SemaphoreType.DMA((4,)),
        pltpu.SemaphoreType.REGULAR((NZ,)),
    ]
    outs = pl.pallas_call(
        kernel,
        out_shape=(
            shape((rows, channels), BF16),
            shape((rows, channels), BF16),
            shape((rows, channels), BF16),
            shape((16, channels), F32),
            shape((rows, channels), F32),
        ),
        in_specs=[vmem] * 5 + [pl.BlockSpec(memory_space=pltpu.SMEM)] + [vmem] * 7,
        out_specs=[vmem] * 5,
        scratch_shapes=scratch,
        compiler_params=pltpu.CompilerParams(
            collective_id=0, has_side_effects=True, vmem_limit_bytes=48 * 1024 * 1024
        ),
    )(
        query_in[0], key_in[0], value_in[0], cotangent[0], long_filter,
        short_taps.reshape(9, channels), *(jnp.asarray(t) for t in tables()),
    )
    grad_query, grad_key, grad_value, grad_taps, grad_filter = outs
    return (
        grad_query[None], grad_key[None], grad_value[None],
        grad_taps[:9].reshape(short_taps.shape), grad_filter,
    )


def solution(mesh):
    seq = P("dp", "ctx", None)
    return jax.shard_map(
        per_device,
        mesh=mesh,
        in_specs=(seq, seq, seq, P(), P("ctx", None), seq),
        out_specs=(seq, seq, seq, P(), P("ctx", None)),
        check_vma=False,
    )
```

```python
import functools
import math

import jax
import jax.numpy as jnp
import numpy as np
from jax import lax
from jax.experimental import pallas as pl
from jax.experimental.pallas import tpu as pltpu
from jax.sharding import PartitionSpec as P

MESH = pl.DeviceIdType.MESH
F32 = jnp.float32
BF16 = jnp.bfloat16

NZ, NPLANE, NCTX = 8, 16, 64
GROUP = NZ * NPLANE
CHAN = 4
SEQ = 2
POS = 128
ROWS = 16


def split_np(table):
    high = table.astype(jnp.bfloat16)
    low = (table - high.astype(np.float64)).astype(jnp.bfloat16)
    return high, low


@functools.cache
def tables():
    length = NCTX * POS
    a = np.arange(NCTX, dtype=np.float64)
    b = np.arange(POS, dtype=np.float64)
    outer = 2 * np.pi * np.outer(a, a + 0.25) / NCTX
    turn = 2 * np.pi * np.outer(a + 0.25, b) / length
    inner = 2 * np.pi * (np.outer(b, b) % POS) / POS
    first = np.concatenate([np.cos(outer.T), -np.sin(outer.T)], axis=0)
    high, low = split_np(first)
    first_cat = np.concatenate([high, low, high], axis=1)
    scale = 1.0 / (length * math.sqrt(length))
    last = np.concatenate([np.cos(outer), -np.sin(outer)], axis=1) * scale
    high, low = split_np(last)
    last_cat = np.concatenate([high, low, high], axis=1)
    c, s = np.cos(inner), np.sin(inner)
    forward = np.stack(split_np(np.block([[c, -s], [s, c]])))
    inverse = np.stack(split_np(np.block([[c, s], [-s, c]])))
    twiddle = np.stack([np.cos(turn), np.sin(turn)]).astype(np.float32)
    pick = np.zeros((32, 4, CHAN, 4, POS), np.float32)
    for g in range(32):
        for f in range(4):
            for i in range(CHAN):
                pick[g, f, i, f, CHAN * g + i] = 1
    pick = pick.reshape(512, 512).astype(jnp.bfloat16)
    return first_cat, last_cat, forward, inverse, twiddle, pick


def split(x):
    high = x.astype(BF16)
    return high, (x - high.astype(F32)).astype(BF16)


def dot(a, b):
    return jnp.dot(a, b, preferred_element_type=F32)


def dot_nt(a, b):
    return lax.dot_general(a, b, (((1,), (1,)), ((), ())), preferred_element_type=F32)


def stack_split(x):
    high, low = split(x)
    return jnp.concatenate([high, high, low], axis=0)


def wide_dot(x, table):
    high, low = split(x)
    return dot(high, table[0]) + (dot(high, table[1]) + dot(low, table[0]))


def wrap(v, n):
    return jnp.where(v >= n, v - n, v)


def kernel(
    q_hbm, k_hbm, v_hbm, c_hbm, filt_hbm, taps_hbm, first_hbm, last_hbm, fwd_hbm, inv_hbm, tw_hbm, pick_hbm,
    rrecv, tap_recv,
    q_ref, k_ref, v_ref, c_ref, filt_ref, taps_ref, first_ref, last_ref, fwd_ref, inv_ref, tw_ref, pick_ref,
    send_buf, recv_buf, fsend, frecv, raw, fraw, spec, hspec, keep, pack, rsend,
    sib_send, sib_recv, tap_rows, tap_own, tap_sib, tap_send,
    load_sems, send_sem, recv_sem, fsend_sem, frecv_sem, rsend_sem, rrecv_sem,
    sib_sems, tap_sems, plane_sem,
):
    dp, cx = lax.axis_index("dp"), lax.axis_index("ctx")
    zh, core = dp // 2, lax.rem(dp, 2)
    y, zl, x = cx // 16, lax.rem(cx // 4, 4), lax.rem(cx, 4)
    z = zh * 4 + zl
    me = zh * NCTX + cx
    xs = [wrap(x + dx, 4) for dx in range(4)]

    def place(zt, yt, xt, core_t):
        half = zt // 4
        ctx = yt * 16 + (zt - 4 * half) * 4 + xt
        return (half * 2 + core_t, ctx), half * NCTX + ctx

    def over(planes, act):
        bases = []
        for zt, own in planes:
            half = zt // 4
            bases.append((half * 2 + core, (zt - 4 * half) * 4, half * NCTX, own))

        def row(dy, carry, skip=False):
            yt = wrap(y + dy, 4) * 16
            for dx in range(4):
                for n, (dp_t, zrow, owner, own) in enumerate(bases):
                    if own and skip and dx == 0:
                        continue
                    ctx = yt + zrow + xs[dx]
                    act(n, (dp_t, ctx), owner + ctx)
            return carry

        if any(own for _, own in planes):
            row(0, 0, True)
            lax.fori_loop(1, 4, row, 0)
        else:
            lax.fori_loop(0, 4, row, 0)

    def plane_of(k):
        return wrap(z + k, NZ)

    sibling = (zh * 2 + (1 - core), cx)

    barrier = pltpu.get_barrier_semaphore()

    def signal_to(device, sem):
        pl.semaphore_signal(sem, inc=1, device_id=device, device_id_type=MESH)

    columns = [place(plane_of(k), y, x, core)[0] for k in range(NZ)]
    for k in (4, 3, 5, 2, 6, 1, 7):
        signal_to(columns[k], barrier)
    over([(z, True)], lambda n, to, owner: signal_to(to, barrier))
    signal_to(sibling, barrier)

    loads = [
        pltpu.make_async_copy(source, target, load_sems.at[n])
        for n, (source, target) in enumerate([
            (pick_hbm, pick_ref), (q_hbm, q_ref), (k_hbm, k_ref), (v_hbm, v_ref), (c_hbm, c_ref),
            (filt_hbm, filt_ref), (first_hbm, first_ref), (fwd_hbm, fwd_ref), (tw_hbm, tw_ref),
            (taps_hbm, taps_ref), (inv_hbm, inv_ref), (last_hbm, last_ref),
        ])
    ]
    for load in loads:
        load.start()
    for load in loads[:5]:
        load.wait()

    for j in range(4):
        lanes = slice(j * POS, (j + 1) * POS)
        fields = jnp.concatenate([q_ref[:, lanes], k_ref[:, lanes], v_ref[:, lanes], c_ref[:, lanes]], axis=1)
        rows = dot_nt(pick_ref[...], fields).astype(BF16)
        send_buf[pl.ds(j * 32, 32)] = rows.reshape(32, ROWS, POS)
    loads[5].wait()
    for j in range(4):
        lanes = slice(j * POS, (j + 1) * POS)
        high, low = split(filt_ref[:, lanes])
        pick_one = pick_ref[:, :POS]
        rows = dot_nt(pick_one, high) + dot_nt(pick_one, low)
        fsend[pl.ds(j * 32, 32)] = rows.reshape(32, ROWS, POS)[:, :CHAN, :]

    own = pltpu.make_async_copy(send_buf.at[me], recv_buf.at[me], recv_sem.at[zh])
    own.start()
    fown = pltpu.make_async_copy(fsend.at[me], frecv.at[cx], frecv_sem)
    fown.start()

    pl.semaphore_wait(barrier, NPLANE - 1 + NZ - 1 + 1)
    for k in (4, 3, 5, 2, 6, 1, 7):
        signal_to(columns[k], plane_sem.at[NZ - k])

    near = (0, 1, 2, 7)
    for planes in ((0,), (7, 1), (6, 2), (5, 3), (4,)):
        for k in planes:
            if k:
                pl.semaphore_wait(plane_sem.at[k], 1)

        def send(n, to, owner, planes=planes):
            if planes[n] in near:
                pltpu.make_async_remote_copy(
                    src_ref=fsend.at[owner], dst_ref=frecv.at[cx], send_sem=fsend_sem, recv_sem=frecv_sem,
                    device_id=to, device_id_type=MESH,
                ).start()
            pltpu.make_async_remote_copy(
                src_ref=send_buf.at[owner], dst_ref=recv_buf.at[me], send_sem=send_sem, recv_sem=recv_sem.at[zh],
                device_id=to, device_id_type=MESH,
            ).start()

        over([(plane_of(k), k == 0) for k in planes], send)

    def wait_bytes(ref, sem):
        pltpu.make_async_copy(ref, ref, sem).wait()

    row_id = lax.broadcasted_iota(jnp.int32, (NCTX, POS), 0)
    lane_id = lax.broadcasted_iota(jnp.int32, (NCTX, POS), 1)

    def before(v, s):
        turned = pltpu.roll(v, s, 1)
        carried = jnp.where(row_id == 0, 0.0, pltpu.roll(turned, 1, 0))
        return jnp.where(lane_id < s, carried, turned)

    def after(v, s):
        turned = pltpu.roll(v, POS - s, 1)
        carried = jnp.where(row_id == NCTX - 1, 0.0, pltpu.roll(turned, NCTX - 1, 0))
        return jnp.where(lane_id >= POS - s, carried, turned)

    for load in loads[6:]:
        load.wait()
    channel = lax.broadcasted_iota(jnp.int32, (3, GROUP * CHAN), 1)
    tap_values = [
        [jnp.sum(jnp.where(channel == me * CHAN + i, taps_ref[branch], 0.0), axis=1, keepdims=True) for i in range(CHAN)]
        for branch in range(3)
    ]

    def tap(branch, j, i):
        return tap_values[branch][i][j:j + 1]

    def field(h, f, i):
        return raw[h, pl.ds(f * CHAN + i, NCTX, ROWS), :]

    cos, sin = tw_ref[0], tw_ref[1]

    def spectrum(values):
        turned = dot(first_ref[...], stack_split(jnp.concatenate(values, axis=1)))
        parts = []
        for n in range(len(values)):
            re, im = turned[:NCTX, n * POS:(n + 1) * POS], turned[NCTX:, n * POS:(n + 1) * POS]
            parts.append(jnp.concatenate([re * cos + im * sin, im * cos - re * sin], axis=1))
        return wide_dot(jnp.concatenate(parts, axis=0), fwd_ref)

    def signal(spectra):
        joined = jnp.concatenate([jnp.concatenate(s, axis=1) for s in spectra], axis=0)
        turned = wide_dot(joined, inv_ref)
        parts = []
        for n in range(len(spectra)):
            re, im = turned[n * NCTX:(n + 1) * NCTX, :POS], turned[n * NCTX:(n + 1) * NCTX, POS:]
            parts.append(jnp.concatenate([re * cos - im * sin, re * sin + im * cos], axis=0))
        return dot(last_ref[...], stack_split(jnp.concatenate(parts, axis=1)))

    def halves(ref, n):
        return ref[n * NCTX:(n + 1) * NCTX, :POS], ref[n * NCTX:(n + 1) * NCTX, POS:]

    for h in (zh, 1 - zh):
        wait_bytes(recv_buf.at[pl.ds(h * NCTX, NCTX)], recv_sem.at[h])
        raw[h] = recv_buf[pl.ds(h * NCTX, NCTX)].astype(F32).reshape(NCTX * ROWS, POS)
        values = []
        for i in range(CHAN):
            feats = []
            for branch in range(3):
                v = field(h, branch, i)
                feats.append(
                    tap(branch, 0, i) * v + tap(branch, 1, i) * before(v, 1) + tap(branch, 2, i) * before(v, 2)
                )
            keep[h, i, 0] = feats[1]
            keep[h, i, 1] = feats[2]
            values += [feats[1] * feats[2], feats[0] * field(h, 3, i)]
        spec[h] = spectrum(values)

    corrs = []
    for i in range(CHAN):
        re = im = 0.0
        for h in range(SEQ):
            mr, mi = halves(spec.at[h], 2 * i)
            gr, gi = halves(spec.at[h], 2 * i + 1)
            re, im = re + (mr * gr + mi * gi), im + (mr * gi - mi * gr)
        corrs.append((re, im))
    sib_send[...] = signal(corrs)
    sib = pltpu.make_async_remote_copy(
        src_ref=sib_send, dst_ref=sib_recv, send_sem=sib_sems.at[0], recv_sem=sib_sems.at[1],
        device_id=sibling, device_id_type=MESH,
    )
    sib.start()

    wait_bytes(frecv, frecv_sem)
    filt = frecv[...]
    fraw[...] = jnp.concatenate([filt, jnp.zeros_like(filt)], axis=1).reshape(NCTX * 8, POS)
    hspec[...] = spectrum([fraw[pl.ds(i, NCTX, 8), :] for i in range(CHAN)])

    tap_rows[...] = jnp.zeros_like(tap_rows)
    for step, h in enumerate((1 - zh, zh)):
        spectra = []
        for i in range(CHAN):
            fr, fi = halves(hspec, i)
            mr, mi = halves(spec.at[h], 2 * i)
            gr, gi = halves(spec.at[h], 2 * i + 1)
            spectra += [(fr * mr - fi * mi, fr * mi + fi * mr), (fr * gr + fi * gi, fr * gi - fi * gr)]
        back = signal(spectra)
        grads = []
        for i in range(CHAN):
            conv = back[:, 2 * i * POS:(2 * i + 1) * POS]
            adj = back[:, (2 * i + 1) * POS:(2 * i + 2) * POS]
            grads.append([field(h, 3, i) * conv, adj * keep[h, i, 1], adj * keep[h, i, 0]])
            for branch in range(3):
                d = grads[i][branch]
                pack[pl.ds(branch * CHAN + i, NCTX, ROWS), :] = (
                    tap(branch, 0, i) * d + tap(branch, 1, i) * after(d, 1) + tap(branch, 2, i) * after(d, 2)
                )
        if step == 0:
            sib.wait_recv()
            for i in range(CHAN):
                pack[pl.ds(3 * CHAN + i, NCTX, ROWS), :] = (
                    sib_send[:, i * POS:(i + 1) * POS] + sib_recv[:, i * POS:(i + 1) * POS]
                )
        rsend[pl.ds(h * NCTX, NCTX)] = pack[...].reshape(NCTX, ROWS, POS).astype(BF16)

        def give(n, to, owner):
            pltpu.make_async_remote_copy(
                src_ref=rsend.at[owner], dst_ref=rrecv.at[me], send_sem=rsend_sem, recv_sem=rrecv_sem,
                device_id=to, device_id_type=MESH,
            ).start()

        over([(h * 4 + wrap(zl + t, 4), step == 1 and t == 0) for t in range(4)], give)
        for i in range(CHAN):
            for branch in range(3):
                d, v = grads[i][branch], field(h, branch, i)
                for j in range(3):
                    term = d * (before(v, j) if j else v)
                    row = (branch * 3 + j) * CHAN + i
                    tap_rows[row:row + 1, :] += jnp.sum(term, axis=0, keepdims=True)
    rown = pltpu.make_async_copy(rsend.at[me], rrecv.at[me], rrecv_sem)
    rown.start()

    ones = jnp.ones((8, POS), F32)
    scale = 1.0 / math.sqrt(SEQ * 2 * NCTX * POS)
    sums = lax.dot_general(
        ones, tap_rows[...], (((1,), (1,)), ((), ())), precision=lax.Precision.HIGHEST, preferred_element_type=F32
    )
    tap_own[...] = sums[0:1] * scale
    tap_sibling = pltpu.make_async_remote_copy(
        src_ref=tap_own, dst_ref=tap_sib, send_sem=tap_sems.at[0], recv_sem=tap_sems.at[1],
        device_id=sibling, device_id_type=MESH,
    )
    tap_sibling.start()
    tap_sibling.wait_recv()
    tap_send[...] = tap_own[...] + tap_sib[...]
    town = pltpu.make_async_copy(tap_send, tap_recv.at[me], tap_sems.at[3])
    town.start()

    def tell(n, to, owner):
        pltpu.make_async_remote_copy(
            src_ref=tap_send, dst_ref=tap_recv.at[me], send_sem=tap_sems.at[2], recv_sem=tap_sems.at[3],
            device_id=to, device_id_type=MESH,
        ).start()

    over([((1 - zh) * 4 + wrap(zl + t, 4), False) for t in range(4)], tell)
    over([(zh * 4 + wrap(zl + t, 4), t == 0) for t in range(4)], tell)

    wait_bytes(send_buf.at[pl.ds(0, GROUP - 1)], send_sem)
    wait_bytes(fsend.at[pl.ds(0, NCTX - 1)], fsend_sem)
    sib.wait_send()
    tap_sibling.wait_send()

    wait_bytes(rrecv, rrecv_sem)
    wait_bytes(tap_recv, tap_sems.at[3])
    wait_bytes(rsend.at[pl.ds(0, GROUP - 1)], rsend_sem)
    wait_bytes(tap_recv.at[pl.ds(0, GROUP - 1)], tap_sems.at[2])


def finish(
    rows_hbm, taps_hbm, pick_hbm, gq_hbm, gk_hbm, gv_hbm, gt_hbm, gf_hbm,
    rows_ref, taps_ref, pick_ref, gq_ref, gk_ref, gv_ref, gt_ref, gf_ref, load_sems, out_sems,
):
    load_pick = pltpu.make_async_copy(pick_hbm, pick_ref, load_sems.at[0])
    load_pick.start()
    loads = [
        pltpu.make_async_copy(rows_hbm.at[pl.ds(j * 32, 32)], rows_ref.at[pl.ds(j * 32, 32)], load_sems.at[1 + j])
        for j in range(4)
    ]
    for load in loads:
        load.start()
    load_taps = pltpu.make_async_copy(taps_hbm, taps_ref, load_sems.at[5])
    load_taps.start()
    load_pick.wait()
    outs = []
    for j in range(4):
        lanes = pl.ds(j * POS, POS)
        loads[j].wait()
        rows = rows_ref[pl.ds(j * 32, 32)].reshape(512, POS)
        out = lax.dot_general(rows, pick_ref[...], (((0,), (0,)), ((), ())), preferred_element_type=F32)
        gq_ref[:, lanes] = out[:, :POS].astype(BF16)
        gk_ref[:, lanes] = out[:, POS:2 * POS].astype(BF16)
        gv_ref[:, lanes] = out[:, 2 * POS:3 * POS].astype(BF16)
        gf_ref[:, lanes] = out[:, 3 * POS:]
        for n, (source, target) in enumerate([(gq_ref, gq_hbm), (gk_ref, gk_hbm), (gv_ref, gv_hbm), (gf_ref, gf_hbm)]):
            outs.append(pltpu.make_async_copy(source.at[:, lanes], target.at[:, lanes], out_sems.at[4 * j + n]))
            outs[-1].start()

    load_taps.wait()
    taps_all = taps_ref[...].reshape(GROUP, POS)
    total = jnp.zeros((16, GROUP * CHAN), F32)
    for i in range(CHAN):
        pick_row = (
            lax.broadcasted_iota(jnp.int32, (16, POS), 1)
            == CHAN * lax.broadcasted_iota(jnp.int32, (16, POS), 0) + i
        ).astype(F32)
        spread = (
            lax.broadcasted_iota(jnp.int32, (GROUP, GROUP * CHAN), 1)
            == CHAN * lax.broadcasted_iota(jnp.int32, (GROUP, GROUP * CHAN), 0) + i
        ).astype(F32)
        rows = lax.dot_general(
            pick_row, taps_all, (((1,), (1,)), ((), ())),
            precision=lax.Precision.HIGHEST, preferred_element_type=F32,
        )
        total += jnp.dot(rows, spread, precision=lax.Precision.HIGHEST, preferred_element_type=F32)
    for branch in range(3):
        gt_ref[branch] = total[branch * 3:branch * 3 + 3]
    outs.append(pltpu.make_async_copy(gt_ref, gt_hbm, out_sems.at[16]))
    outs[-1].start()
    for out in outs:
        out.wait()


def per_device(query_in, key_in, value_in, short_taps, long_filter, cotangent):
    rows, channels = query_in.shape[1:]
    hbm = pl.BlockSpec(memory_space=pltpu.HBM)
    shape = jax.ShapeDtypeStruct
    results = (
        shape((rows, channels), BF16),
        shape((rows, channels), BF16),
        shape((rows, channels), BF16),
        shape(short_taps.shape, F32),
        shape((rows, channels), F32),
    )
    constants = [jnp.asarray(t) for t in tables()]
    operands = [query_in[0], key_in[0], value_in[0], cotangent[0], long_filter, short_taps, *constants]
    scratch = [pltpu.VMEM(v.shape, v.dtype) for v in operands] + [
        pltpu.VMEM((GROUP, ROWS, POS), BF16),
        pltpu.VMEM((GROUP, ROWS, POS), BF16),
        pltpu.VMEM((GROUP, CHAN, POS), F32),
        pltpu.VMEM((NCTX, CHAN, POS), F32),
        pltpu.VMEM((SEQ, NCTX * ROWS, POS), F32),
        pltpu.VMEM((NCTX * 8, POS), F32),
        pltpu.VMEM((SEQ, 2 * CHAN * NCTX, 2 * POS), F32),
        pltpu.VMEM((CHAN * NCTX, 2 * POS), F32),
        pltpu.VMEM((SEQ, CHAN, 2, NCTX, POS), F32),
        pltpu.VMEM((NCTX * ROWS, POS), F32),
        pltpu.VMEM((GROUP, ROWS, POS), BF16),
        pltpu.VMEM((NCTX, CHAN * POS), F32),
        pltpu.VMEM((NCTX, CHAN * POS), F32),
        pltpu.VMEM((POS, POS), F32),
        pltpu.VMEM((1, POS), F32),
        pltpu.VMEM((1, POS), F32),
        pltpu.VMEM((1, POS), F32),
        pltpu.SemaphoreType.DMA((len(operands),)),
        pltpu.SemaphoreType.DMA,
        pltpu.SemaphoreType.DMA((SEQ,)),
        pltpu.SemaphoreType.DMA,
        pltpu.SemaphoreType.DMA,
        pltpu.SemaphoreType.DMA,
        pltpu.SemaphoreType.DMA,
        pltpu.SemaphoreType.DMA((2,)),
        pltpu.SemaphoreType.DMA((4,)),
        pltpu.SemaphoreType.REGULAR((NZ,)),
    ]
    params = functools.partial(pltpu.CompilerParams, vmem_limit_bytes=63 * 1024 * 1024)
    held = pl.pallas_call(
        kernel,
        out_shape=(shape((GROUP, ROWS, POS), BF16), shape((GROUP, 1, POS), F32)),
        in_specs=[hbm] * len(operands),
        out_specs=[hbm] * 2,
        scratch_shapes=scratch,
        compiler_params=params(collective_id=0, has_side_effects=True),
    )(*operands)
    inner = [*held, operands[-1]]
    grad_query, grad_key, grad_value, grad_taps, grad_filter = pl.pallas_call(
        finish,
        out_shape=results,
        in_specs=[hbm] * 3,
        out_specs=[hbm] * 5,
        scratch_shapes=[pltpu.VMEM(v.shape, v.dtype) for v in (*inner, *results)]
        + [pltpu.SemaphoreType.DMA((6,)), pltpu.SemaphoreType.DMA((17,))],
        compiler_params=params(),
    )(*inner)
    return (grad_query[None], grad_key[None], grad_value[None], grad_taps, grad_filter)


def solution(mesh):
    seq = P("dp", "ctx", None)
    return jax.shard_map(
        per_device,
        mesh=mesh,
        in_specs=(seq, seq, seq, P(), P("ctx", None), seq),
        out_specs=(seq, seq, seq, P(), P("ctx", None)),
        check_vma=False,
    )
```

```python
import functools
import itertools
import math

import jax
import jax.numpy as jnp
import numpy as np
from jax import lax
from jax.experimental import pallas as pl
from jax.experimental.pallas import tpu as pltpu
from jax.sharding import PartitionSpec as P

MESH = pl.DeviceIdType.MESH
F32 = jnp.float32
BF16 = jnp.bfloat16

NZ, NPLANE, NCTX = 8, 16, 64
GROUP = NZ * NPLANE
CHAN = 4
SEQ = 2
POS = 128
ROWS = 16
REACH = 8


def shell(reach):
    hops = lambda d, n: min(d, n - d)
    by_z = [
        [(dx, dy, dz) for dy in range(4) for dx in range(4) if hops(dx, 4) + hops(dy, 4) + hops(dz, NZ) == reach]
        for dz in (4, 3, 5, 2, 6, 1, 7, 0)
    ]
    return [d for row in itertools.zip_longest(*by_z) for d in row if d]


def split_np(table):
    high = table.astype(jnp.bfloat16)
    low = (table - high.astype(np.float64)).astype(jnp.bfloat16)
    return high, low


@functools.cache
def tables():
    length = NCTX * POS
    a = np.arange(NCTX, dtype=np.float64)
    b = np.arange(POS, dtype=np.float64)
    outer = 2 * np.pi * np.outer(a, a + 0.25) / NCTX
    turn = 2 * np.pi * np.outer(a + 0.25, b) / length
    inner = 2 * np.pi * (np.outer(b, b) % POS) / POS
    first = np.concatenate([np.cos(outer.T), -np.sin(outer.T)], axis=0)
    high, low = split_np(first)
    first_cat = np.concatenate([high, low, high], axis=1)
    scale = 1.0 / (length * math.sqrt(length))
    last = np.concatenate([np.cos(outer), -np.sin(outer)], axis=1) * scale
    high, low = split_np(last)
    last_cat = np.concatenate([high, low, high], axis=1)
    c, s = np.cos(inner), np.sin(inner)
    forward = np.stack(split_np(np.block([[c, -s], [s, c]])))
    inverse = np.stack(split_np(np.block([[c, s], [-s, c]])))
    twiddle = np.stack([np.cos(turn), np.sin(turn)]).astype(np.float32)
    pick = np.zeros((32, 4, CHAN, 4, POS), np.float32)
    for g in range(32):
        for f in range(4):
            for i in range(CHAN):
                pick[g, f, i, f, CHAN * g + i] = 1
    pick = pick.reshape(512, 512).astype(jnp.bfloat16)
    return first_cat, last_cat, forward, inverse, twiddle, pick


def split(x):
    high = x.astype(BF16)
    return high, (x - high.astype(F32)).astype(BF16)


def dot(a, b):
    return jnp.dot(a, b, preferred_element_type=F32)


def dot_nt(a, b):
    return lax.dot_general(a, b, (((1,), (1,)), ((), ())), preferred_element_type=F32)


def stack_split(x):
    high, low = split(x)
    return jnp.concatenate([high, high, low], axis=0)


def wide_dot(x, table):
    high, low = split(x)
    return dot(high, table[0]) + (dot(high, table[1]) + dot(low, table[0]))


def wrap(v, n):
    return jnp.where(v >= n, v - n, v)


def kernel(
    q_hbm, k_hbm, v_hbm, c_hbm, filt_hbm, taps_hbm, first_hbm, last_hbm, fwd_hbm, inv_hbm, tw_hbm, pick_hbm,
    rrecv, tap_recv,
    q_ref, k_ref, v_ref, c_ref, filt_ref, taps_ref, first_ref, last_ref, fwd_ref, inv_ref, tw_ref, pick_ref,
    send_buf, recv_buf, fsend, frecv, raw, fraw, spec, hspec, keep, pack, rsend,
    sib_send, sib_recv, tap_rows, tap_own, tap_sib, tap_send,
    load_sems, send_sem, recv_sem, fsend_sem, frecv_sem, rsend_sem, rrecv_sem,
    sib_sems, tap_sems, plane_sem,
):
    dp, cx = lax.axis_index("dp"), lax.axis_index("ctx")
    zh, core = dp // 2, lax.rem(dp, 2)
    y, zl, x = cx // 16, lax.rem(cx // 4, 4), lax.rem(cx, 4)
    z = zh * 4 + zl
    me = zh * NCTX + cx

    def place(zt, yt, xt, core_t):
        half = zt // 4
        ctx = yt * 16 + (zt - 4 * half) * 4 + xt
        return (half * 2 + core_t, ctx), half * NCTX + ctx

    def over(planes, act):
        bases = []
        for zt, own in planes:
            half = zt // 4
            bases.append((half * 2 + core, (zt - 4 * half) * 4, half * NCTX, own))

        def row(dy, carry, skip=False):
            yt = wrap(y + dy, 4) * 16
            for dx in (2, 1, 3, 0):
                for n, (dp_t, zrow, owner, own) in enumerate(bases):
                    if own and skip and dx == 0:
                        continue
                    ctx = yt + zrow + xs[dx]
                    act(n, (dp_t, ctx), owner + ctx)
            return carry

        if any(own for _, own in planes):
            row(0, 0, True)
            lax.fori_loop(1, 4, row, 0)
        else:
            lax.fori_loop(0, 4, row, 0)

    def plane_of(k):
        return wrap(z + k, NZ)

    sibling = (zh * 2 + (1 - core), cx)

    barrier = pltpu.get_barrier_semaphore()

    def signal_to(device, sem):
        pl.semaphore_signal(sem, inc=1, device_id=device, device_id_type=MESH)

    xs = [wrap(x + dx, 4) for dx in range(4)]
    ys = [wrap(y + dy, 4) * 16 for dy in range(4)]
    zs = []
    for dz in range(NZ):
        zt = plane_of(dz)
        half = zt // 4
        zs.append((half * 2 + core, (zt - 4 * half) * 4, half * NCTX))

    def target(dx, dy, dz):
        dp_t, zrow, first = zs[dz]
        ctx = ys[dy] + zrow + xs[dx]
        return (dp_t, ctx), first + ctx

    columns = [target(0, 0, dz)[0] for dz in range(NZ)]
    for dz in (4, 3, 5, 2, 6, 1, 7):
        signal_to(columns[dz], barrier)
    for dy in (2, 1, 3, 0):
        for dx in (2, 1, 3, 0):
            if dx or dy:
                signal_to(target(dx, dy, 0)[0], barrier)
    signal_to(sibling, barrier)

    loads = [
        pltpu.make_async_copy(source, target, load_sems.at[n])
        for n, (source, target) in enumerate([
            (pick_hbm, pick_ref), (q_hbm, q_ref), (k_hbm, k_ref), (v_hbm, v_ref), (c_hbm, c_ref),
            (filt_hbm, filt_ref), (first_hbm, first_ref), (fwd_hbm, fwd_ref), (tw_hbm, tw_ref),
            (taps_hbm, taps_ref), (inv_hbm, inv_ref), (last_hbm, last_ref),
        ])
    ]
    for load in loads:
        load.start()
    for load in loads[:5]:
        load.wait()

    for j in range(4):
        lanes = slice(j * POS, (j + 1) * POS)
        fields = jnp.concatenate([q_ref[:, lanes], k_ref[:, lanes], v_ref[:, lanes], c_ref[:, lanes]], axis=1)
        rows = dot_nt(pick_ref[...], fields).astype(BF16)
        send_buf[pl.ds(j * 32, 32)] = rows.reshape(32, ROWS, POS)
    loads[5].wait()
    for j in range(4):
        lanes = slice(j * POS, (j + 1) * POS)
        rows = dot_nt(pick_ref[:, :POS], filt_ref[:, lanes].astype(BF16)).astype(BF16)
        fsend[pl.ds(j * 32, 32)] = rows.reshape(32, ROWS, POS)[:, :CHAN, :]

    own = pltpu.make_async_copy(send_buf.at[me], recv_buf.at[me], recv_sem.at[zh])
    own.start()
    fown = pltpu.make_async_copy(fsend.at[me], frecv.at[cx], frecv_sem)
    fown.start()

    pl.semaphore_wait(barrier, NPLANE - 1 + NZ - 1 + 1)
    for dz in (4, 3, 5, 2, 6, 1, 7):
        signal_to(columns[dz], plane_sem.at[NZ - dz])
    near = (0, 1, 2, 7)
    plane = [(dx, dy) for dy in (2, 1, 3, 0) for dx in (2, 1, 3, 0)]
    for dz in range(1, NZ):
        pl.semaphore_wait(plane_sem.at[dz], 1)
    for dx, dy in plane:
        for d in [(dx, dy, dz) for dz in (4, 3, 5, 2, 6, 1, 7, 0) if dx or dy or dz]:
            to, owner = target(*d)
            pltpu.make_async_remote_copy(
                src_ref=send_buf.at[owner], dst_ref=recv_buf.at[me], send_sem=send_sem, recv_sem=recv_sem.at[zh],
                device_id=to, device_id_type=MESH,
            ).start()
            if d[2] in near:
                pltpu.make_async_remote_copy(
                    src_ref=fsend.at[owner], dst_ref=frecv.at[cx], send_sem=fsend_sem, recv_sem=frecv_sem,
                    device_id=to, device_id_type=MESH,
                ).start()

    def wait_bytes(ref, sem):
        pltpu.make_async_copy(ref, ref, sem).wait()

    row_id = lax.broadcasted_iota(jnp.int32, (NCTX, POS), 0)
    lane_id = lax.broadcasted_iota(jnp.int32, (NCTX, POS), 1)

    def before(v, s):
        turned = pltpu.roll(v, s, 1)
        carried = jnp.where(row_id == 0, 0.0, pltpu.roll(turned, 1, 0))
        return jnp.where(lane_id < s, carried, turned)

    def after(v, s):
        turned = pltpu.roll(v, POS - s, 1)
        carried = jnp.where(row_id == NCTX - 1, 0.0, pltpu.roll(turned, NCTX - 1, 0))
        return jnp.where(lane_id >= POS - s, carried, turned)

    for load in loads[6:]:
        load.wait()
    channel = lax.broadcasted_iota(jnp.int32, (3, GROUP * CHAN), 1)
    tap_values = [
        [jnp.sum(jnp.where(channel == me * CHAN + i, taps_ref[branch], 0.0), axis=1, keepdims=True) for i in range(CHAN)]
        for branch in range(3)
    ]

    def tap(branch, j, i):
        return tap_values[branch][i][j:j + 1]

    def field(h, f, i):
        return raw[h, pl.ds(f * CHAN + i, NCTX, ROWS), :]

    cos, sin = tw_ref[0], tw_ref[1]

    def spectrum(values):
        turned = dot(first_ref[...], stack_split(jnp.concatenate(values, axis=1)))
        parts = []
        for n in range(len(values)):
            re, im = turned[:NCTX, n * POS:(n + 1) * POS], turned[NCTX:, n * POS:(n + 1) * POS]
            parts.append(jnp.concatenate([re * cos + im * sin, im * cos - re * sin], axis=1))
        return wide_dot(jnp.concatenate(parts, axis=0), fwd_ref)

    def signal(spectra):
        joined = jnp.concatenate([jnp.concatenate(s, axis=1) for s in spectra], axis=0)
        turned = wide_dot(joined, inv_ref)
        parts = []
        for n in range(len(spectra)):
            re, im = turned[n * NCTX:(n + 1) * NCTX, :POS], turned[n * NCTX:(n + 1) * NCTX, POS:]
            parts.append(jnp.concatenate([re * cos - im * sin, re * sin + im * cos], axis=0))
        return dot(last_ref[...], stack_split(jnp.concatenate(parts, axis=1)))

    def halves(ref, n):
        return ref[n * NCTX:(n + 1) * NCTX, :POS], ref[n * NCTX:(n + 1) * NCTX, POS:]

    wait_bytes(frecv, frecv_sem)
    filt = frecv[...].astype(F32)
    fraw[...] = jnp.concatenate([filt, jnp.zeros_like(filt)], axis=1).reshape(NCTX * 8, POS)
    hspec[...] = spectrum([fraw[pl.ds(i, NCTX, 8), :] for i in range(CHAN)])

    for h in (zh, 1 - zh):
        wait_bytes(recv_buf.at[pl.ds(h * NCTX, NCTX)], recv_sem.at[h])
        raw[h] = recv_buf[pl.ds(h * NCTX, NCTX)].astype(F32).reshape(NCTX * ROWS, POS)
        values = []
        for i in range(CHAN):
            feats = []
            for branch in range(3):
                v = field(h, branch, i)
                feats.append(
                    tap(branch, 0, i) * v + tap(branch, 1, i) * before(v, 1) + tap(branch, 2, i) * before(v, 2)
                )
            keep[h, i, 0] = feats[1]
            keep[h, i, 1] = feats[2]
            values += [feats[1] * feats[2], feats[0] * field(h, 3, i)]
        spec[h] = spectrum(values)

    corrs = []
    for i in range(CHAN):
        re = im = 0.0
        for h in range(SEQ):
            mr, mi = halves(spec.at[h], 2 * i)
            gr, gi = halves(spec.at[h], 2 * i + 1)
            re, im = re + (mr * gr + mi * gi), im + (mr * gi - mi * gr)
        corrs.append((re, im))
    sib_send[...] = signal(corrs)
    sib = pltpu.make_async_remote_copy(
        src_ref=sib_send, dst_ref=sib_recv, send_sem=sib_sems.at[0], recv_sem=sib_sems.at[1],
        device_id=sibling, device_id_type=MESH,
    )
    sib.start()

    tap_rows[...] = jnp.zeros_like(tap_rows)
    for step, h in enumerate((1 - zh, zh)):
        spectra = []
        for i in range(CHAN):
            fr, fi = halves(hspec, i)
            mr, mi = halves(spec.at[h], 2 * i)
            gr, gi = halves(spec.at[h], 2 * i + 1)
            spectra += [(fr * mr - fi * mi, fr * mi + fi * mr), (fr * gr + fi * gi, fr * gi - fi * gr)]
        back = signal(spectra)
        grads = []
        for i in range(CHAN):
            conv = back[:, 2 * i * POS:(2 * i + 1) * POS]
            adj = back[:, (2 * i + 1) * POS:(2 * i + 2) * POS]
            grads.append([field(h, 3, i) * conv, adj * keep[h, i, 1], adj * keep[h, i, 0]])
            for branch in range(3):
                d = grads[i][branch]
                pack[pl.ds(branch * CHAN + i, NCTX, ROWS), :] = (
                    tap(branch, 0, i) * d + tap(branch, 1, i) * after(d, 1) + tap(branch, 2, i) * after(d, 2)
                )
        if step == 0:
            sib.wait_recv()
            for i in range(CHAN):
                pack[pl.ds(3 * CHAN + i, NCTX, ROWS), :] = (
                    sib_send[:, i * POS:(i + 1) * POS] + sib_recv[:, i * POS:(i + 1) * POS]
                )
        def tap_terms():
            for i in range(CHAN):
                for branch in range(3):
                    d, v = grads[i][branch], field(h, branch, i)
                    for j in range(3):
                        term = d * (before(v, j) if j else v)
                        row = (branch * 3 + j) * CHAN + i
                        tap_rows[row:row + 1, :] += jnp.sum(term, axis=0, keepdims=True)

        def give(n, to, owner):
            pltpu.make_async_remote_copy(
                src_ref=rsend.at[owner], dst_ref=rrecv.at[me], send_sem=rsend_sem, recv_sem=rrecv_sem,
                device_id=to, device_id_type=MESH,
            ).start()

        def give_all():
            rsend[pl.ds(h * NCTX, NCTX)] = pack[...].reshape(NCTX, ROWS, POS).astype(BF16)
            over([(h * 4 + wrap(zl + t, 4), step == 1 and t == 0) for t in range(4)], give)

        if step == 0:
            give_all()
            tap_terms()
        else:
            tap_terms()
            ones = jnp.ones((8, POS), BF16)
            scale = 1.0 / math.sqrt(SEQ * 2 * NCTX * POS)
            high, low = split(tap_rows[...])
            tap_own[...] = (dot_nt(ones, high) + dot_nt(ones, low))[0:1] * scale
            tap_sibling = pltpu.make_async_remote_copy(
                src_ref=tap_own, dst_ref=tap_sib, send_sem=tap_sems.at[0], recv_sem=tap_sems.at[1],
                device_id=sibling, device_id_type=MESH,
            )
            tap_sibling.start()
            give_all()
    tap_sibling.wait_recv()
    tap_send[...] = tap_own[...] + tap_sib[...]
    for dy in (2, 1, 3, 0):
        for dx in (2, 1, 3, 0):
            for dz in (4, 3, 5, 2, 6, 1, 7, 0):
                if dx or dy or dz:
                    pltpu.make_async_remote_copy(
                        src_ref=tap_send, dst_ref=tap_recv.at[me], send_sem=tap_sems.at[2], recv_sem=tap_sems.at[3],
                        device_id=target(dx, dy, dz)[0], device_id_type=MESH,
                    ).start()
    town = pltpu.make_async_copy(tap_send, tap_recv.at[me], tap_sems.at[3])
    town.start()
    rown = pltpu.make_async_copy(rsend.at[me], rrecv.at[me], rrecv_sem)
    rown.start()

    wait_bytes(send_buf.at[pl.ds(0, GROUP - 1)], send_sem)
    wait_bytes(fsend.at[pl.ds(0, NCTX - 1)], fsend_sem)
    sib.wait_send()
    tap_sibling.wait_send()

    wait_bytes(rrecv, rrecv_sem)
    wait_bytes(tap_recv, tap_sems.at[3])
    wait_bytes(rsend.at[pl.ds(0, GROUP - 1)], rsend_sem)
    wait_bytes(tap_recv.at[pl.ds(0, GROUP - 1)], tap_sems.at[2])


def finish(
    rows_hbm, taps_hbm, pick_hbm, gq_hbm, gk_hbm, gv_hbm, gt_hbm, gf_hbm,
    rows_ref, taps_ref, pick_ref, gq_ref, gk_ref, gv_ref, gt_ref, gf_ref, load_sems, out_sems,
):
    load_pick = pltpu.make_async_copy(pick_hbm, pick_ref, load_sems.at[0])
    load_pick.start()
    loads = [
        pltpu.make_async_copy(rows_hbm.at[pl.ds(j * 32, 32)], rows_ref.at[pl.ds(j * 32, 32)], load_sems.at[1 + j])
        for j in range(4)
    ]
    for load in loads:
        load.start()
    load_taps = pltpu.make_async_copy(taps_hbm, taps_ref, load_sems.at[5])
    load_taps.start()
    row = lax.broadcasted_iota(jnp.int32, (CHAN * 16, POS), 0)
    lane = lax.broadcasted_iota(jnp.int32, (CHAN * 16, POS), 1)
    pick_row = (lane == CHAN * (row % 16) + row // 16).astype(F32).astype(BF16)
    row = lax.broadcasted_iota(jnp.int32, (CHAN * GROUP, GROUP * CHAN), 0)
    lane = lax.broadcasted_iota(jnp.int32, (CHAN * GROUP, GROUP * CHAN), 1)
    spread = (lane == CHAN * (row % GROUP) + row // GROUP).astype(F32).astype(BF16)
    load_pick.wait()
    outs = []
    for j in range(4):
        lanes = pl.ds(j * POS, POS)
        loads[j].wait()
        rows = rows_ref[pl.ds(j * 32, 32)].reshape(512, POS)
        out = lax.dot_general(rows, pick_ref[...], (((0,), (0,)), ((), ())), preferred_element_type=F32)
        gq_ref[:, lanes] = out[:, :POS].astype(BF16)
        gk_ref[:, lanes] = out[:, POS:2 * POS].astype(BF16)
        gv_ref[:, lanes] = out[:, 2 * POS:3 * POS].astype(BF16)
        gf_ref[:, lanes] = out[:, 3 * POS:]
        for n, (source, target) in enumerate([(gq_ref, gq_hbm), (gk_ref, gk_hbm), (gv_ref, gv_hbm), (gf_ref, gf_hbm)]):
            outs.append(pltpu.make_async_copy(source.at[:, lanes], target.at[:, lanes], out_sems.at[4 * j + n]))
            outs[-1].start()

    load_taps.wait()
    high, low = split(taps_ref[...].reshape(GROUP, POS))
    rows = dot_nt(pick_row, high) + dot_nt(pick_row, low)
    high, low = split(jnp.concatenate([rows[i * 16:(i + 1) * 16] for i in range(CHAN)], axis=1))
    both = dot(jnp.concatenate([high, low], axis=0), spread)
    total = both[:16] + both[16:]
    for branch in range(3):
        gt_ref[branch] = total[branch * 3:branch * 3 + 3]
    outs.append(pltpu.make_async_copy(gt_ref, gt_hbm, out_sems.at[16]))
    outs[-1].start()
    for out in outs:
        out.wait()


def per_device(query_in, key_in, value_in, short_taps, long_filter, cotangent):
    rows, channels = query_in.shape[1:]
    hbm = pl.BlockSpec(memory_space=pltpu.HBM)
    shape = jax.ShapeDtypeStruct
    results = (
        shape((rows, channels), BF16),
        shape((rows, channels), BF16),
        shape((rows, channels), BF16),
        shape(short_taps.shape, F32),
        shape((rows, channels), F32),
    )
    constants = [jnp.asarray(t) for t in tables()]
    operands = [query_in[0], key_in[0], value_in[0], cotangent[0], long_filter, short_taps, *constants]
    scratch = [pltpu.VMEM(v.shape, v.dtype) for v in operands] + [
        pltpu.VMEM((GROUP, ROWS, POS), BF16),
        pltpu.VMEM((GROUP, ROWS, POS), BF16),
        pltpu.VMEM((GROUP, CHAN, POS), BF16),
        pltpu.VMEM((NCTX, CHAN, POS), BF16),
        pltpu.VMEM((SEQ, NCTX * ROWS, POS), F32),
        pltpu.VMEM((NCTX * 8, POS), F32),
        pltpu.VMEM((SEQ, 2 * CHAN * NCTX, 2 * POS), F32),
        pltpu.VMEM((CHAN * NCTX, 2 * POS), F32),
        pltpu.VMEM((SEQ, CHAN, 2, NCTX, POS), F32),
        pltpu.VMEM((NCTX * ROWS, POS), F32),
        pltpu.VMEM((GROUP, ROWS, POS), BF16),
        pltpu.VMEM((NCTX, CHAN * POS), F32),
        pltpu.VMEM((NCTX, CHAN * POS), F32),
        pltpu.VMEM((POS, POS), F32),
        pltpu.VMEM((1, POS), F32),
        pltpu.VMEM((1, POS), F32),
        pltpu.VMEM((1, POS), F32),
        pltpu.SemaphoreType.DMA((len(operands),)),
        pltpu.SemaphoreType.DMA,
        pltpu.SemaphoreType.DMA((SEQ,)),
        pltpu.SemaphoreType.DMA,
        pltpu.SemaphoreType.DMA,
        pltpu.SemaphoreType.DMA,
        pltpu.SemaphoreType.DMA,
        pltpu.SemaphoreType.DMA((2,)),
        pltpu.SemaphoreType.DMA((4,)),
        pltpu.SemaphoreType.REGULAR((NZ,)),
    ]
    params = functools.partial(pltpu.CompilerParams, vmem_limit_bytes=63 * 1024 * 1024)
    held = pl.pallas_call(
        kernel,
        out_shape=(shape((GROUP, ROWS, POS), BF16), shape((GROUP, 1, POS), F32)),
        in_specs=[hbm] * len(operands),
        out_specs=[hbm] * 2,
        scratch_shapes=scratch,
        compiler_params=params(collective_id=0, has_side_effects=True),
    )(*operands)
    inner = [*held, operands[-1]]
    grad_query, grad_key, grad_value, grad_taps, grad_filter = pl.pallas_call(
        finish,
        out_shape=results,
        in_specs=[hbm] * 3,
        out_specs=[hbm] * 5,
        scratch_shapes=[pltpu.VMEM(v.shape, v.dtype) for v in (*inner, *results)]
        + [pltpu.SemaphoreType.DMA((6,)), pltpu.SemaphoreType.DMA((17,))],
        compiler_params=params(),
    )(*inner)
    return (grad_query[None], grad_key[None], grad_value[None], grad_taps, grad_filter)


def solution(mesh):
    seq = P("dp", "ctx", None)
    return jax.shard_map(
        per_device,
        mesh=mesh,
        in_specs=(seq, seq, seq, P(), P("ctx", None), seq),
        out_specs=(seq, seq, seq, P(), P("ctx", None)),
        check_vma=False,
    )
```

```python
import functools
import math

import jax
import jax.numpy as jnp
import numpy as np
from jax import lax
from jax.experimental import pallas as pl
from jax.experimental.pallas import tpu as pltpu
from jax.sharding import PartitionSpec as P

MESH = pl.DeviceIdType.MESH
F32 = jnp.float32
BF16 = jnp.bfloat16

NZ, NPLANE, NCTX = 8, 16, 64
GROUP = NZ * NPLANE
CHAN = 4
SEQ = 2
POS = 128
PARTS = 2
PAIR = CHAN // PARTS
ROWS = 4 * PAIR


def split_np(table):
    high = table.astype(jnp.bfloat16)
    low = (table - high.astype(np.float64)).astype(jnp.bfloat16)
    return high, low


@functools.cache
def tables():
    length = NCTX * POS
    a = np.arange(NCTX, dtype=np.float64)
    b = np.arange(POS, dtype=np.float64)
    outer = 2 * np.pi * np.outer(a, a + 0.25) / NCTX
    turn = 2 * np.pi * np.outer(a + 0.25, b) / length
    inner = 2 * np.pi * (np.outer(b, b) % POS) / POS
    first = np.concatenate([np.cos(outer.T), -np.sin(outer.T)], axis=0)
    high, low = split_np(first)
    first_cat = np.concatenate([high, low, high], axis=1)
    scale = 1.0 / (length * math.sqrt(length))
    last = np.concatenate([np.cos(outer), -np.sin(outer)], axis=1) * scale
    high, low = split_np(last)
    last_cat = np.concatenate([high, low, high], axis=1)
    c, s = np.cos(inner), np.sin(inner)
    forward = np.stack(split_np(np.block([[c, -s], [s, c]])))
    inverse = np.stack(split_np(np.block([[c, s], [-s, c]])))
    twiddle = np.stack([np.cos(turn), np.sin(turn)]).astype(np.float32)
    pick = np.zeros((PARTS, 32, 4, PAIR, 4, POS), np.float32)
    pick_one = np.zeros((32, 8, POS), np.float32)
    for g in range(32):
        for i in range(CHAN):
            pick_one[g, i, CHAN * g + i] = 1
            for f in range(4):
                pick[i // PAIR, g, f, i % PAIR, f, CHAN * g + i] = 1
    pick = pick.reshape(512, 512).astype(jnp.bfloat16)
    pick_one = pick_one.reshape(256, POS).astype(jnp.bfloat16)
    return first_cat, last_cat, forward, inverse, twiddle, pick_one, pick


def split(x):
    high = x.astype(BF16)
    return high, (x - high.astype(F32)).astype(BF16)


def dot(a, b):
    return jnp.dot(a, b, preferred_element_type=F32)


def dot_nt(a, b):
    return lax.dot_general(a, b, (((1,), (1,)), ((), ())), preferred_element_type=F32)


def stack_split(x):
    high, low = split(x)
    return jnp.concatenate([high, high, low], axis=0)


def wide_dot(x, table):
    high, low = split(x)
    return dot(high, table[0]) + (dot(high, table[1]) + dot(low, table[0]))


def wrap(v, n):
    return jnp.where(v >= n, v - n, v)


def kernel(
    q_hbm, k_hbm, v_hbm, c_hbm, filt_hbm, taps_hbm, first_hbm, last_hbm, fwd_hbm, inv_hbm, tw_hbm, pick1_hbm, pick_hbm,
    rrecv, tap_recv,
    q_ref, k_ref, v_ref, c_ref, filt_ref, taps_ref, first_ref, last_ref, fwd_ref, inv_ref, tw_ref, pick1_ref, pick_ref,
    send_buf, recv_buf, fsend, frecv, raw, fraw, spec, hspec, keep, pack, rsend,
    sib_send, sib_recv, tap_rows, tap_own, tap_sib, tap_send,
    load_sems, send_sem, recv_sem, fsend_sem, frecv_sem, rsend_sem, rrecv_sem,
    sib_sems, tap_sems, plane_sem,
):
    dp, cx = lax.axis_index("dp"), lax.axis_index("ctx")
    zh, core = dp // 2, lax.rem(dp, 2)
    y, zl, x = cx // 16, lax.rem(cx // 4, 4), lax.rem(cx, 4)
    z = zh * 4 + zl
    me = zh * NCTX + cx

    def plane_of(k):
        return wrap(z + k, NZ)

    sibling = (zh * 2 + (1 - core), cx)

    barrier = pltpu.get_barrier_semaphore()

    def signal_to(device, sem):
        pl.semaphore_signal(sem, inc=1, device_id=device, device_id_type=MESH)

    xs = [wrap(x + dx, 4) for dx in range(4)]
    ys = [wrap(y + dy, 4) * 16 for dy in range(4)]
    zs = []
    for dz in range(NZ):
        zt = plane_of(dz)
        half = zt // 4
        zs.append((half * 2 + core, (zt - 4 * half) * 4, half * NCTX))

    def target(dx, dy, dz):
        dp_t, zrow, first = zs[dz]
        ctx = ys[dy] + zrow + xs[dx]
        return (dp_t, ctx), first + ctx

    columns = [target(0, 0, dz)[0] for dz in range(NZ)]
    for dz in (4, 3, 5, 2, 6, 1, 7):
        signal_to(columns[dz], barrier)
    for dy in (2, 1, 3, 0):
        for dx in (2, 1, 3, 0):
            if dx or dy:
                signal_to(target(dx, dy, 0)[0], barrier)
    signal_to(sibling, barrier)

    loads = [
        pltpu.make_async_copy(source, target, load_sems.at[n])
        for n, (source, target) in enumerate([
            (pick_hbm, pick_ref), (q_hbm, q_ref), (k_hbm, k_ref), (v_hbm, v_ref), (c_hbm, c_ref),
            (filt_hbm, filt_ref), (pick1_hbm, pick1_ref), (first_hbm, first_ref), (fwd_hbm, fwd_ref), (tw_hbm, tw_ref),
            (taps_hbm, taps_ref), (inv_hbm, inv_ref), (last_hbm, last_ref),
        ])
    ]
    for load in loads:
        load.start()
    for load in loads[:5]:
        load.wait()

    for j in range(4):
        lanes = slice(j * POS, (j + 1) * POS)
        fields = jnp.concatenate([q_ref[:, lanes], k_ref[:, lanes], v_ref[:, lanes], c_ref[:, lanes]], axis=1)
        rows = dot_nt(pick_ref[...], fields).astype(BF16)
        send_buf[:, pl.ds(j * 32, 32)] = rows.reshape(PARTS, 32, ROWS, POS)
    loads[5].wait()
    loads[6].wait()
    for j in range(4):
        lanes = slice(j * POS, (j + 1) * POS)
        rows = dot_nt(pick1_ref[...], filt_ref[:, lanes].astype(BF16))
        fsend[pl.ds(j * 32, 32)] = rows.reshape(32, 8, POS)[:, :CHAN, :].astype(BF16)

    for part in range(PARTS):
        pltpu.make_async_copy(send_buf.at[part, me], recv_buf.at[part, me], recv_sem.at[part]).start()
    fown = pltpu.make_async_copy(fsend.at[me], frecv.at[cx], frecv_sem)
    fown.start()

    pl.semaphore_wait(barrier, NPLANE - 1 + NZ - 1 + 1)
    for dz in (4, 3, 5, 2, 6, 1, 7):
        signal_to(columns[dz], plane_sem.at[NZ - dz])
    near = (0, 1, 2, 7)
    others = [
        (dx, dy, dz)
        for dy in (2, 1, 3, 0) for dx in (2, 1, 3, 0) for dz in (4, 3, 5, 2, 6, 1, 7, 0) if dx or dy or dz
    ]
    for dz in range(1, NZ):
        pl.semaphore_wait(plane_sem.at[dz], 1)
    for part in range(PARTS):
        for d in others:
            to, owner = target(*d)
            pltpu.make_async_remote_copy(
                src_ref=send_buf.at[part, owner], dst_ref=recv_buf.at[part, me],
                send_sem=send_sem.at[part], recv_sem=recv_sem.at[part], device_id=to, device_id_type=MESH,
            ).start()
            if part == 0 and d[2] in near:
                pltpu.make_async_remote_copy(
                    src_ref=fsend.at[owner], dst_ref=frecv.at[cx], send_sem=fsend_sem, recv_sem=frecv_sem,
                    device_id=to, device_id_type=MESH,
                ).start()

    def wait_bytes(ref, sem):
        pltpu.make_async_copy(ref, ref, sem).wait()

    row_id = lax.broadcasted_iota(jnp.int32, (NCTX, POS), 0)
    lane_id = lax.broadcasted_iota(jnp.int32, (NCTX, POS), 1)

    def before(v, s):
        turned = pltpu.roll(v, s, 1)
        carried = jnp.where(row_id == 0, 0.0, pltpu.roll(turned, 1, 0))
        return jnp.where(lane_id < s, carried, turned)

    def after(v, s):
        turned = pltpu.roll(v, POS - s, 1)
        carried = jnp.where(row_id == NCTX - 1, 0.0, pltpu.roll(turned, NCTX - 1, 0))
        return jnp.where(lane_id >= POS - s, carried, turned)

    for load in loads[7:]:
        load.wait()
    channel = lax.broadcasted_iota(jnp.int32, (3, GROUP * CHAN), 1)
    tap_values = [
        [jnp.sum(jnp.where(channel == me * CHAN + i, taps_ref[branch], 0.0), axis=1, keepdims=True) for i in range(CHAN)]
        for branch in range(3)
    ]

    def tap(branch, j, i):
        return tap_values[branch][i][j:j + 1]

    def field(h, f, i):
        return raw[pl.ds(h * NCTX * ROWS + f * PAIR + i, NCTX, ROWS), :]

    cos, sin = tw_ref[0], tw_ref[1]

    def spectrum(values):
        turned = dot(first_ref[...], stack_split(jnp.concatenate(values, axis=1)))
        parts = []
        for n in range(len(values)):
            re, im = turned[:NCTX, n * POS:(n + 1) * POS], turned[NCTX:, n * POS:(n + 1) * POS]
            parts.append(jnp.concatenate([re * cos + im * sin, im * cos - re * sin], axis=1))
        return wide_dot(jnp.concatenate(parts, axis=0), fwd_ref)

    def signal(spectra):
        joined = jnp.concatenate([jnp.concatenate(s, axis=1) for s in spectra], axis=0)
        turned = wide_dot(joined, inv_ref)
        parts = []
        for n in range(len(spectra)):
            re, im = turned[n * NCTX:(n + 1) * NCTX, :POS], turned[n * NCTX:(n + 1) * NCTX, POS:]
            parts.append(jnp.concatenate([re * cos - im * sin, re * sin + im * cos], axis=0))
        return dot(last_ref[...], stack_split(jnp.concatenate(parts, axis=1)))

    def halves(ref, n):
        return ref[n * NCTX:(n + 1) * NCTX, :POS], ref[n * NCTX:(n + 1) * NCTX, POS:]

    wait_bytes(frecv, frecv_sem)
    filt = frecv[...].astype(F32)
    fraw[...] = jnp.concatenate([filt, jnp.zeros_like(filt)], axis=1).reshape(NCTX * 8, POS)
    hspec[...] = spectrum([fraw[pl.ds(i, NCTX, 8), :] for i in range(CHAN)])

    tap_rows[...] = jnp.zeros_like(tap_rows)
    pairs = [(h, i) for h in range(SEQ) for i in range(PAIR)]
    for part in range(PARTS):
        wait_bytes(recv_buf.at[part], recv_sem.at[part])
        raw[...] = recv_buf[part].astype(F32).reshape(GROUP * ROWS, POS)
        values = []
        for n, (h, i) in enumerate(pairs):
            feats = []
            for branch in range(3):
                v = field(h, branch, i)
                c = part * PAIR + i
                feats.append(
                    tap(branch, 0, c) * v + tap(branch, 1, c) * before(v, 1) + tap(branch, 2, c) * before(v, 2)
                )
            keep[n, 0] = feats[1]
            keep[n, 1] = feats[2]
            values += [feats[1] * feats[2], feats[0] * field(h, 3, i)]
        spec[...] = spectrum(values)

        corrs = []
        for i in range(PAIR):
            re = im = 0.0
            for h in range(SEQ):
                n = h * PAIR + i
                mr, mi = halves(spec, 2 * n)
                gr, gi = halves(spec, 2 * n + 1)
                re, im = re + (mr * gr + mi * gi), im + (mr * gi - mi * gr)
            corrs.append((re, im))
        sib_send[part] = signal(corrs)
        sib = pltpu.make_async_remote_copy(
            src_ref=sib_send.at[part], dst_ref=sib_recv.at[part],
            send_sem=sib_sems.at[0, part], recv_sem=sib_sems.at[1, part], device_id=sibling, device_id_type=MESH,
        )
        sib.start()

        spectra = []
        for n, (h, i) in enumerate(pairs):
            fr, fi = halves(hspec, part * PAIR + i)
            mr, mi = halves(spec, 2 * n)
            gr, gi = halves(spec, 2 * n + 1)
            spectra += [(fr * mr - fi * mi, fr * mi + fi * mr), (fr * gr + fi * gi, fr * gi - fi * gr)]
        back = signal(spectra)
        grads = []
        for n, (h, i) in enumerate(pairs):
            conv = back[:, 2 * n * POS:(2 * n + 1) * POS]
            adj = back[:, (2 * n + 1) * POS:(2 * n + 2) * POS]
            grads.append([field(h, 3, i) * conv, adj * keep[n, 1], adj * keep[n, 0]])
            c = part * PAIR + i
            for branch in range(3):
                d = grads[n][branch]
                pack[pl.ds(h * NCTX * ROWS + branch * PAIR + i, NCTX, ROWS), :] = (
                    tap(branch, 0, c) * d + tap(branch, 1, c) * after(d, 1) + tap(branch, 2, c) * after(d, 2)
                )

        def tap_terms():
            for n, (h, i) in enumerate(pairs):
                for branch in range(3):
                    d, v = grads[n][branch], field(h, branch, i)
                    for j in range(3):
                        term = d * (before(v, j) if j else v)
                        row = (branch * 3 + j) * CHAN + part * PAIR + i
                        tap_rows[row:row + 1, :] += jnp.sum(term, axis=0, keepdims=True)

        def give():
            sib.wait()
            for i in range(PAIR):
                total = sib_send[part, :, i * POS:(i + 1) * POS] + sib_recv[part, :, i * POS:(i + 1) * POS]
                for h in range(SEQ):
                    pack[pl.ds(h * NCTX * ROWS + 3 * PAIR + i, NCTX, ROWS), :] = total
            rsend[part] = pack[...].reshape(GROUP, ROWS, POS).astype(BF16)
            for d in others:
                to, owner = target(*d)
                pltpu.make_async_remote_copy(
                    src_ref=rsend.at[part, owner], dst_ref=rrecv.at[part, me],
                    send_sem=rsend_sem.at[part], recv_sem=rrecv_sem.at[part], device_id=to, device_id_type=MESH,
                ).start()
            pltpu.make_async_copy(rsend.at[part, me], rrecv.at[part, me], rrecv_sem.at[part]).start()

        if part < PARTS - 1:
            give()
            tap_terms()
        else:
            tap_terms()
            ones = jnp.ones((8, POS), BF16)
            scale = 1.0 / math.sqrt(SEQ * 2 * NCTX * POS)
            high, low = split(tap_rows[...])
            tap_own[...] = (dot_nt(ones, high) + dot_nt(ones, low))[0:1] * scale
            tap_sibling = pltpu.make_async_remote_copy(
                src_ref=tap_own, dst_ref=tap_sib, send_sem=tap_sems.at[0], recv_sem=tap_sems.at[1],
                device_id=sibling, device_id_type=MESH,
            )
            tap_sibling.start()
            give()
    tap_sibling.wait()
    tap_send[...] = tap_own[...] + tap_sib[...]
    for d in others:
        pltpu.make_async_remote_copy(
            src_ref=tap_send, dst_ref=tap_recv.at[me], send_sem=tap_sems.at[2], recv_sem=tap_sems.at[3],
            device_id=target(*d)[0], device_id_type=MESH,
        ).start()
    pltpu.make_async_copy(tap_send, tap_recv.at[me], tap_sems.at[3]).start()

    wait_bytes(fsend.at[pl.ds(0, NCTX - 1)], fsend_sem)
    for part in range(PARTS):
        wait_bytes(send_buf.at[part, pl.ds(0, GROUP - 1)], send_sem.at[part])
    for part in range(PARTS):
        wait_bytes(rsend.at[part, pl.ds(0, GROUP - 1)], rsend_sem.at[part])
    wait_bytes(tap_recv.at[pl.ds(0, GROUP - 1)], tap_sems.at[2])
    for part in range(PARTS):
        wait_bytes(rrecv.at[part], rrecv_sem.at[part])
    wait_bytes(tap_recv, tap_sems.at[3])


def finish(
    rows_hbm, taps_hbm, pick_hbm, gq_hbm, gk_hbm, gv_hbm, gt_hbm, gf_hbm,
    rows_ref, taps_ref, pick_ref, gq_ref, gk_ref, gv_ref, gt_ref, gf_ref, load_sems, out_sems,
):
    load_pick = pltpu.make_async_copy(pick_hbm, pick_ref, load_sems.at[0])
    load_pick.start()
    loads = [
        pltpu.make_async_copy(rows_hbm.at[:, pl.ds(j * 32, 32)], rows_ref.at[:, pl.ds(j * 32, 32)], load_sems.at[1 + j])
        for j in range(4)
    ]
    for load in loads:
        load.start()
    load_taps = pltpu.make_async_copy(taps_hbm, taps_ref, load_sems.at[5])
    load_taps.start()
    row = lax.broadcasted_iota(jnp.int32, (CHAN * 16, POS), 0)
    lane = lax.broadcasted_iota(jnp.int32, (CHAN * 16, POS), 1)
    pick_row = (lane == CHAN * (row % 16) + row // 16).astype(F32).astype(BF16)
    row = lax.broadcasted_iota(jnp.int32, (CHAN * GROUP, GROUP * CHAN), 0)
    lane = lax.broadcasted_iota(jnp.int32, (CHAN * GROUP, GROUP * CHAN), 1)
    spread = (lane == CHAN * (row % GROUP) + row // GROUP).astype(F32).astype(BF16)
    load_pick.wait()
    outs = []
    for j in range(4):
        lanes = pl.ds(j * POS, POS)
        loads[j].wait()
        rows = rows_ref[:, pl.ds(j * 32, 32)].reshape(512, POS)
        out = lax.dot_general(rows, pick_ref[...], (((0,), (0,)), ((), ())), preferred_element_type=F32)
        gq_ref[:, lanes] = out[:, :POS].astype(BF16)
        gk_ref[:, lanes] = out[:, POS:2 * POS].astype(BF16)
        gv_ref[:, lanes] = out[:, 2 * POS:3 * POS].astype(BF16)
        gf_ref[:, lanes] = out[:, 3 * POS:]
        for n, (source, target) in enumerate([(gq_ref, gq_hbm), (gk_ref, gk_hbm), (gv_ref, gv_hbm), (gf_ref, gf_hbm)]):
            outs.append(pltpu.make_async_copy(source.at[:, lanes], target.at[:, lanes], out_sems.at[4 * j + n]))
            outs[-1].start()

    load_taps.wait()
    high, low = split(taps_ref[...].reshape(GROUP, POS))
    rows = dot_nt(pick_row, high) + dot_nt(pick_row, low)
    high, low = split(jnp.concatenate([rows[i * 16:(i + 1) * 16] for i in range(CHAN)], axis=1))
    both = dot(jnp.concatenate([high, low], axis=0), spread)
    total = both[:16] + both[16:]
    for branch in range(3):
        gt_ref[branch] = total[branch * 3:branch * 3 + 3]
    outs.append(pltpu.make_async_copy(gt_ref, gt_hbm, out_sems.at[16]))
    outs[-1].start()
    for out in outs:
        out.wait()


def per_device(query_in, key_in, value_in, short_taps, long_filter, cotangent):
    rows, channels = query_in.shape[1:]
    hbm = pl.BlockSpec(memory_space=pltpu.HBM)
    shape = jax.ShapeDtypeStruct
    results = (
        shape((rows, channels), BF16),
        shape((rows, channels), BF16),
        shape((rows, channels), BF16),
        shape(short_taps.shape, F32),
        shape((rows, channels), F32),
    )
    constants = [jnp.asarray(t) for t in tables()]
    operands = [query_in[0], key_in[0], value_in[0], cotangent[0], long_filter, short_taps, *constants]
    scratch = [pltpu.VMEM(v.shape, v.dtype) for v in operands] + [
        pltpu.VMEM((PARTS, GROUP, ROWS, POS), BF16),
        pltpu.VMEM((PARTS, GROUP, ROWS, POS), BF16),
        pltpu.VMEM((GROUP, CHAN, POS), BF16),
        pltpu.VMEM((NCTX, CHAN, POS), BF16),
        pltpu.VMEM((GROUP * ROWS, POS), F32),
        pltpu.VMEM((NCTX * 8, POS), F32),
        pltpu.VMEM((2 * SEQ * PAIR * NCTX, 2 * POS), F32),
        pltpu.VMEM((CHAN * NCTX, 2 * POS), F32),
        pltpu.VMEM((SEQ * PAIR, 2, NCTX, POS), F32),
        pltpu.VMEM((GROUP * ROWS, POS), F32),
        pltpu.VMEM((PARTS, GROUP, ROWS, POS), BF16),
        pltpu.VMEM((PARTS, NCTX, PAIR * POS), F32),
        pltpu.VMEM((PARTS, NCTX, PAIR * POS), F32),
        pltpu.VMEM((POS, POS), F32),
        pltpu.VMEM((1, POS), F32),
        pltpu.VMEM((1, POS), F32),
        pltpu.VMEM((1, POS), F32),
        pltpu.SemaphoreType.DMA((len(operands),)),
        pltpu.SemaphoreType.DMA((PARTS,)),
        pltpu.SemaphoreType.DMA((PARTS,)),
        pltpu.SemaphoreType.DMA,
        pltpu.SemaphoreType.DMA,
        pltpu.SemaphoreType.DMA((PARTS,)),
        pltpu.SemaphoreType.DMA((PARTS,)),
        pltpu.SemaphoreType.DMA((2, PARTS)),
        pltpu.SemaphoreType.DMA((4,)),
        pltpu.SemaphoreType.REGULAR((NZ,)),
    ]
    params = functools.partial(pltpu.CompilerParams, vmem_limit_bytes=63 * 1024 * 1024)
    held = pl.pallas_call(
        kernel,
        out_shape=(shape((PARTS, GROUP, ROWS, POS), BF16), shape((GROUP, 1, POS), F32)),
        in_specs=[hbm] * len(operands),
        out_specs=[hbm] * 2,
        scratch_shapes=scratch,
        compiler_params=params(collective_id=0, has_side_effects=True),
    )(*operands)
    inner = [*held, operands[-1]]
    grad_query, grad_key, grad_value, grad_taps, grad_filter = pl.pallas_call(
        finish,
        out_shape=results,
        in_specs=[hbm] * 3,
        out_specs=[hbm] * 5,
        scratch_shapes=[pltpu.VMEM(v.shape, v.dtype) for v in (*inner, *results)]
        + [pltpu.SemaphoreType.DMA((6,)), pltpu.SemaphoreType.DMA((17,))],
        compiler_params=params(),
    )(*inner)
    return (grad_query[None], grad_key[None], grad_value[None], grad_taps, grad_filter)


def solution(mesh):
    seq = P("dp", "ctx", None)
    return jax.shard_map(
        per_device,
        mesh=mesh,
        in_specs=(seq, seq, seq, P(), P("ctx", None), seq),
        out_specs=(seq, seq, seq, P(), P("ctx", None)),
        check_vma=False,
    )
```

```python
import functools
import math

import jax
import jax.numpy as jnp
import numpy as np
from jax import lax
from jax.experimental import pallas as pl
from jax.experimental.pallas import tpu as pltpu
from jax.sharding import PartitionSpec as P

MESH = pl.DeviceIdType.MESH
F32 = jnp.float32
BF16 = jnp.bfloat16

NZ, NPLANE, NCTX = 8, 16, 64
GROUP = NZ * NPLANE
CHAN = 4
SEQ = 2
POS = 128
PARTS = 4
PAIR = CHAN // PARTS
ROWS = 4 * PAIR
HELD = 8


def split_np(table):
    high = table.astype(jnp.bfloat16)
    low = (table - high.astype(np.float64)).astype(jnp.bfloat16)
    return high, low


@functools.cache
def tables():
    length = NCTX * POS
    a = np.arange(NCTX, dtype=np.float64)
    b = np.arange(POS, dtype=np.float64)
    outer = 2 * np.pi * np.outer(a, a + 0.25) / NCTX
    turn = 2 * np.pi * np.outer(a + 0.25, b) / length
    inner = 2 * np.pi * (np.outer(b, b) % POS) / POS
    first = np.concatenate([np.cos(outer.T), -np.sin(outer.T)], axis=0)
    high, low = split_np(first)
    first_cat = np.concatenate([high, low, high], axis=1)
    scale = 1.0 / (length * math.sqrt(length))
    last = np.concatenate([np.cos(outer), -np.sin(outer)], axis=1) * scale
    high, low = split_np(last)
    last_cat = np.concatenate([high, low, high], axis=1)
    c, s = np.cos(inner), np.sin(inner)
    forward = np.stack(split_np(np.block([[c, -s], [s, c]])))
    inverse = np.stack(split_np(np.block([[c, s], [-s, c]])))
    twiddle = np.stack([np.cos(turn), np.sin(turn)]).astype(np.float32)
    pick = np.zeros((PARTS, 32, 4, PAIR, 4, POS), np.float32)
    pick_one = np.zeros((32, 8, POS), np.float32)
    for g in range(32):
        for i in range(CHAN):
            pick_one[g, i, CHAN * g + i] = 1
            for f in range(4):
                pick[i // PAIR, g, f, i % PAIR, f, CHAN * g + i] = 1
    back = pick.copy()
    back[:, :, 3] = 0
    back[1:, :, 3] = pick[:-1, :, 3]
    back = np.concatenate([back.reshape(512, 512), pick[-1, :, 3].reshape(32, 512)]).astype(jnp.bfloat16)
    pick = pick.reshape(512, 512).astype(jnp.bfloat16)
    pick_one = pick_one.reshape(256, POS).astype(jnp.bfloat16)
    return (first_cat, last_cat, forward, inverse, twiddle, pick_one, pick), back


def split(x):
    high = x.astype(BF16)
    return high, (x - high.astype(F32)).astype(BF16)


def dot(a, b):
    return jnp.dot(a, b, preferred_element_type=F32)


def dot_nt(a, b):
    return lax.dot_general(a, b, (((1,), (1,)), ((), ())), preferred_element_type=F32)


def stack_split(x):
    high, low = split(x)
    return jnp.concatenate([high, high, low], axis=0)


def wide_dot(x, table):
    high, low = split(x)
    return dot(high, table[0]) + (dot(high, table[1]) + dot(low, table[0]))


def wrap(v, n):
    return jnp.where(v >= n, v - n, v)


def kernel(
    q_hbm, k_hbm, v_hbm, c_hbm, filt_hbm, taps_hbm, first_hbm, last_hbm, fwd_hbm, inv_hbm, tw_hbm, pick1_hbm, pick_hbm,
    rrecv, tap_recv,
    q_ref, k_ref, v_ref, c_ref, filt_ref, taps_ref, first_ref, last_ref, fwd_ref, inv_ref, tw_ref, pick1_ref, pick_ref,
    send_buf, recv_buf, fsend, frecv, raw, fraw, spec, hspec, keep, pack, rsend,
    sib_send, sib_recv, tap_rows, tap_own, tap_sib, tap_send,
    load_sems, send_sem, recv_sem, fsend_sem, frecv_sem, rsend_sem, rrecv_sem,
    sib_sems, tap_sems, plane_sem,
):
    dp, cx = lax.axis_index("dp"), lax.axis_index("ctx")
    zh, core = dp // 2, lax.rem(dp, 2)
    y, zl, x = cx // 16, lax.rem(cx // 4, 4), lax.rem(cx, 4)
    z = zh * 4 + zl
    me = zh * NCTX + cx

    def plane_of(k):
        return wrap(z + k, NZ)

    sibling = (zh * 2 + (1 - core), cx)

    barrier = pltpu.get_barrier_semaphore()

    def signal_to(device, sem):
        pl.semaphore_signal(sem, inc=1, device_id=device, device_id_type=MESH)

    xs = [wrap(x + dx, 4) for dx in range(4)]
    ys = [wrap(y + dy, 4) * 16 for dy in range(4)]
    zs = []
    for dz in range(NZ):
        zt = plane_of(dz)
        half = zt // 4
        zs.append((half * 2 + core, (zt - 4 * half) * 4, half * NCTX))

    def target(dx, dy, dz):
        dp_t, zrow, first = zs[dz]
        ctx = ys[dy] + zrow + xs[dx]
        return (dp_t, ctx), first + ctx

    others = [
        (dx, dy, dz)
        for dz in (4, 3, 5, 2, 6, 1, 7, 0) for dy in (2, 1, 3, 0) for dx in (2, 1, 3, 0) if dx or dy or dz
    ]
    for d in others:
        signal_to(target(*d)[0], barrier)
    signal_to(sibling, barrier)

    loads = [
        pltpu.make_async_copy(source, target, load_sems.at[n])
        for n, (source, target) in enumerate([
            (pick_hbm, pick_ref), (q_hbm, q_ref), (k_hbm, k_ref), (v_hbm, v_ref), (c_hbm, c_ref),
            (filt_hbm, filt_ref), (pick1_hbm, pick1_ref), (first_hbm, first_ref), (fwd_hbm, fwd_ref), (tw_hbm, tw_ref),
            (taps_hbm, taps_ref), (inv_hbm, inv_ref), (last_hbm, last_ref),
        ])
    ]
    for load in loads:
        load.start()
    for load in loads[:5]:
        load.wait()

    for j in range(4):
        lanes = slice(j * POS, (j + 1) * POS)
        fields = jnp.concatenate([q_ref[:, lanes], k_ref[:, lanes], v_ref[:, lanes], c_ref[:, lanes]], axis=1)
        rows = dot_nt(pick_ref[...], fields).astype(BF16)
        send_buf[:, pl.ds(j * 32, 32)] = rows.reshape(PARTS, 32, ROWS, POS)
    loads[5].wait()
    loads[6].wait()
    for j in range(4):
        lanes = slice(j * POS, (j + 1) * POS)
        rows = dot_nt(pick1_ref[...], filt_ref[:, lanes].astype(BF16))
        fsend[pl.ds(j * 32, 32)] = rows.reshape(32, 8, POS)[:, :CHAN, :].astype(BF16)

    for part in range(PARTS):
        pltpu.make_async_copy(send_buf.at[part, me], recv_buf.at[part, me], recv_sem.at[part]).start()
    fown = pltpu.make_async_copy(fsend.at[me], frecv.at[cx], frecv_sem)
    fown.start()

    pl.semaphore_wait(barrier, GROUP)
    near = (0, 1, 2, 7)
    others = [
        (dx, dy, dz)
        for dy in (2, 1, 3, 0) for dx in (2, 1, 3, 0) for dz in (4, 3, 5, 2, 6, 1, 7, 0) if dx or dy or dz
    ]
    for part in range(PARTS):
        for d in others:
            to, owner = target(*d)
            pltpu.make_async_remote_copy(
                src_ref=send_buf.at[part, owner], dst_ref=recv_buf.at[part, me],
                send_sem=send_sem.at[part], recv_sem=recv_sem.at[part], device_id=to, device_id_type=MESH,
            ).start()
            if part == 0 and d[2] in near:
                pltpu.make_async_remote_copy(
                    src_ref=fsend.at[owner], dst_ref=frecv.at[cx], send_sem=fsend_sem, recv_sem=frecv_sem,
                    device_id=to, device_id_type=MESH,
                ).start()

    def wait_bytes(ref, sem):
        pltpu.make_async_copy(ref, ref, sem).wait()

    row_id = lax.broadcasted_iota(jnp.int32, (NCTX, POS), 0)
    lane_id = lax.broadcasted_iota(jnp.int32, (NCTX, POS), 1)

    def before(v, s):
        turned = pltpu.roll(v, s, 1)
        carried = jnp.where(row_id == 0, 0.0, pltpu.roll(turned, 1, 0))
        return jnp.where(lane_id < s, carried, turned)

    def after(v, s):
        turned = pltpu.roll(v, POS - s, 1)
        carried = jnp.where(row_id == NCTX - 1, 0.0, pltpu.roll(turned, NCTX - 1, 0))
        return jnp.where(lane_id >= POS - s, carried, turned)

    for load in loads[7:]:
        load.wait()
    channel = lax.broadcasted_iota(jnp.int32, (3, GROUP * CHAN), 1)
    tap_values = [
        [jnp.sum(jnp.where(channel == me * CHAN + i, taps_ref[branch], 0.0), axis=1, keepdims=True) for i in range(CHAN)]
        for branch in range(3)
    ]

    def tap(branch, j, i):
        return tap_values[branch][i][j:j + 1]

    def field(h, f, i):
        return raw[pl.ds(h * NCTX * HELD + f * PAIR + i, NCTX, HELD), :]

    cos, sin = tw_ref[0], tw_ref[1]

    def spectrum(values):
        turned = dot(first_ref[...], stack_split(jnp.concatenate(values, axis=1)))
        parts = []
        for n in range(len(values)):
            re, im = turned[:NCTX, n * POS:(n + 1) * POS], turned[NCTX:, n * POS:(n + 1) * POS]
            parts.append(jnp.concatenate([re * cos + im * sin, im * cos - re * sin], axis=1))
        return wide_dot(jnp.concatenate(parts, axis=0), fwd_ref)

    def signal(spectra):
        joined = jnp.concatenate([jnp.concatenate(s, axis=1) for s in spectra], axis=0)
        turned = wide_dot(joined, inv_ref)
        parts = []
        for n in range(len(spectra)):
            re, im = turned[n * NCTX:(n + 1) * NCTX, :POS], turned[n * NCTX:(n + 1) * NCTX, POS:]
            parts.append(jnp.concatenate([re * cos - im * sin, re * sin + im * cos], axis=0))
        return dot(last_ref[...], stack_split(jnp.concatenate(parts, axis=1)))

    def halves(ref, n):
        return ref[n * NCTX:(n + 1) * NCTX, :POS], ref[n * NCTX:(n + 1) * NCTX, POS:]

    wait_bytes(frecv, frecv_sem)
    filt = frecv[...].astype(F32)
    fraw[...] = jnp.concatenate([filt, jnp.zeros_like(filt)], axis=1).reshape(NCTX * 8, POS)
    hspec[...] = spectrum([fraw[pl.ds(i, NCTX, 8), :] for i in range(CHAN)])

    tap_rows[...] = jnp.zeros_like(tap_rows)
    pairs = [(h, i) for h in range(SEQ) for i in range(PAIR)]
    sibs = []

    def filter_total(part):
        sibs[part].wait()
        return sib_send[part] + sib_recv[part]

    def filter_rows(part):
        total = filter_total(part)
        for h in range(SEQ):
            pack[pl.ds(h * NCTX * HELD + 3, NCTX, HELD), :] = total

    pack[...] = jnp.zeros_like(pack)
    for part in range(PARTS):
        wait_bytes(recv_buf.at[part], recv_sem.at[part])
        arrived = recv_buf[part].astype(F32)
        raw[...] = jnp.concatenate([arrived, jnp.zeros_like(arrived)], axis=1).reshape(GROUP * HELD, POS)
        values = []
        for n, (h, i) in enumerate(pairs):
            feats = []
            for branch in range(3):
                v = field(h, branch, i)
                c = part * PAIR + i
                feats.append(
                    tap(branch, 0, c) * v + tap(branch, 1, c) * before(v, 1) + tap(branch, 2, c) * before(v, 2)
                )
            keep[n, 0] = feats[1]
            keep[n, 1] = feats[2]
            values += [feats[1] * feats[2], feats[0] * field(h, 3, i)]
        spec[...] = spectrum(values)

        corrs = []
        for i in range(PAIR):
            re = im = 0.0
            for h in range(SEQ):
                n = h * PAIR + i
                mr, mi = halves(spec, 2 * n)
                gr, gi = halves(spec, 2 * n + 1)
                re, im = re + (mr * gr + mi * gi), im + (mr * gi - mi * gr)
            corrs.append((re, im))
        sib_send[part] = signal(corrs)
        sib = pltpu.make_async_remote_copy(
            src_ref=sib_send.at[part], dst_ref=sib_recv.at[part],
            send_sem=sib_sems.at[0, part], recv_sem=sib_sems.at[1, part], device_id=sibling, device_id_type=MESH,
        )
        sib.start()
        sibs.append(sib)

        spectra = []
        for n, (h, i) in enumerate(pairs):
            fr, fi = halves(hspec, part * PAIR + i)
            mr, mi = halves(spec, 2 * n)
            gr, gi = halves(spec, 2 * n + 1)
            spectra += [(fr * mr - fi * mi, fr * mi + fi * mr), (fr * gr + fi * gi, fr * gi - fi * gr)]
        back = signal(spectra)
        grads = []
        for n, (h, i) in enumerate(pairs):
            conv = back[:, 2 * n * POS:(2 * n + 1) * POS]
            adj = back[:, (2 * n + 1) * POS:(2 * n + 2) * POS]
            grads.append([field(h, 3, i) * conv, adj * keep[n, 1], adj * keep[n, 0]])
            c = part * PAIR + i
            for branch in range(3):
                d = grads[n][branch]
                pack[pl.ds(h * NCTX * HELD + branch * PAIR + i, NCTX, HELD), :] = (
                    tap(branch, 0, c) * d + tap(branch, 1, c) * after(d, 1) + tap(branch, 2, c) * after(d, 2)
                )

        def tap_terms():
            for n, (h, i) in enumerate(pairs):
                for branch in range(3):
                    d, v = grads[n][branch], field(h, branch, i)
                    for j in range(3):
                        term = d * (before(v, j) if j else v)
                        row = (branch * 3 + j) * CHAN + part * PAIR + i
                        tap_rows[row:row + 1, :] += jnp.sum(term, axis=0, keepdims=True)

        def give():
            if part:
                filter_rows(part - 1)
            rsend[part] = pack[...].reshape(GROUP, HELD, POS)[:, :ROWS, :].astype(BF16)
            for d in others:
                to, owner = target(*d)
                pltpu.make_async_remote_copy(
                    src_ref=rsend.at[part, owner], dst_ref=rrecv.at[part, me],
                    send_sem=rsend_sem.at[part], recv_sem=rrecv_sem.at[part], device_id=to, device_id_type=MESH,
                ).start()
            pltpu.make_async_copy(rsend.at[part, me], rrecv.at[part, me], rrecv_sem.at[part]).start()

        if part < PARTS - 1:
            give()
            tap_terms()
        else:
            tap_terms()
            ones = jnp.ones((8, POS), BF16)
            scale = 1.0 / math.sqrt(SEQ * 2 * NCTX * POS)
            high, low = split(tap_rows[...])
            tap_own[...] = (dot_nt(ones, high) + dot_nt(ones, low))[0:1] * scale
            tap_sibling = pltpu.make_async_remote_copy(
                src_ref=tap_own, dst_ref=tap_sib, send_sem=tap_sems.at[0], recv_sem=tap_sems.at[1],
                device_id=sibling, device_id_type=MESH,
            )
            tap_sibling.start()
            give()
    tap_sibling.wait()
    total = filter_total(PARTS - 1).reshape(NCTX, 1, POS)
    for h in range(SEQ):
        tap_send[pl.ds(h * NCTX, NCTX), 0:1, :] = total
    tap_send[:, 1:2, :] = jnp.broadcast_to((tap_own[...] + tap_sib[...]).reshape(1, 1, POS), (GROUP, 1, POS))
    for d in others:
        to, owner = target(*d)
        pltpu.make_async_remote_copy(
            src_ref=tap_send.at[owner], dst_ref=tap_recv.at[me], send_sem=tap_sems.at[2], recv_sem=tap_sems.at[3],
            device_id=to, device_id_type=MESH,
        ).start()
    pltpu.make_async_copy(tap_send.at[me], tap_recv.at[me], tap_sems.at[3]).start()

    wait_bytes(fsend.at[pl.ds(0, NCTX - 1)], fsend_sem)
    for part in range(PARTS):
        wait_bytes(send_buf.at[part, pl.ds(0, GROUP - 1)], send_sem.at[part])
    for part in range(PARTS):
        wait_bytes(rsend.at[part, pl.ds(0, GROUP - 1)], rsend_sem.at[part])
    wait_bytes(tap_recv.at[pl.ds(0, GROUP - 1)], tap_sems.at[2])
    for part in range(PARTS):
        wait_bytes(rrecv.at[part], rrecv_sem.at[part])
    wait_bytes(tap_recv, tap_sems.at[3])


def finish(
    rows_hbm, taps_hbm, pick_hbm, gq_hbm, gk_hbm, gv_hbm, gt_hbm, gf_hbm,
    rows_ref, taps_ref, pick_ref, gq_ref, gk_ref, gv_ref, gt_ref, gf_ref, load_sems, out_sems,
):
    load_pick = pltpu.make_async_copy(pick_hbm, pick_ref, load_sems.at[0])
    load_pick.start()
    loads = [
        pltpu.make_async_copy(rows_hbm.at[:, pl.ds(j * 32, 32)], rows_ref.at[:, pl.ds(j * 32, 32)], load_sems.at[1 + j])
        for j in range(4)
    ]
    for load in loads:
        load.start()
    load_taps = pltpu.make_async_copy(taps_hbm, taps_ref, load_sems.at[5])
    load_taps.start()
    row = lax.broadcasted_iota(jnp.int32, (CHAN * 16, POS), 0)
    lane = lax.broadcasted_iota(jnp.int32, (CHAN * 16, POS), 1)
    pick_row = (lane == CHAN * (row % 16) + row // 16).astype(F32).astype(BF16)
    row = lax.broadcasted_iota(jnp.int32, (CHAN * GROUP, GROUP * CHAN), 0)
    lane = lax.broadcasted_iota(jnp.int32, (CHAN * GROUP, GROUP * CHAN), 1)
    spread = (lane == CHAN * (row % GROUP) + row // GROUP).astype(F32).astype(BF16)
    load_pick.wait()
    load_taps.wait()
    outs = []
    for j in range(4):
        lanes = pl.ds(j * POS, POS)
        loads[j].wait()
        rows = jnp.concatenate([
            rows_ref[:, pl.ds(j * 32, 32)].reshape(512, POS),
            taps_ref[pl.ds(j * 32, 32), 0, :].astype(BF16),
        ], axis=0)
        out = lax.dot_general(rows, pick_ref[...], (((0,), (0,)), ((), ())), preferred_element_type=F32)
        gq_ref[:, lanes] = out[:, :POS].astype(BF16)
        gk_ref[:, lanes] = out[:, POS:2 * POS].astype(BF16)
        gv_ref[:, lanes] = out[:, 2 * POS:3 * POS].astype(BF16)
        gf_ref[:, lanes] = out[:, 3 * POS:]
        for n, (source, target) in enumerate([(gq_ref, gq_hbm), (gk_ref, gk_hbm), (gv_ref, gv_hbm), (gf_ref, gf_hbm)]):
            outs.append(pltpu.make_async_copy(source.at[:, lanes], target.at[:, lanes], out_sems.at[4 * j + n]))
            outs[-1].start()

    high, low = split(taps_ref[:, 1, :])
    rows = dot_nt(pick_row, high) + dot_nt(pick_row, low)
    high, low = split(jnp.concatenate([rows[i * 16:(i + 1) * 16] for i in range(CHAN)], axis=1))
    both = dot(jnp.concatenate([high, low], axis=0), spread)
    total = both[:16] + both[16:]
    for branch in range(3):
        gt_ref[branch] = total[branch * 3:branch * 3 + 3]
    outs.append(pltpu.make_async_copy(gt_ref, gt_hbm, out_sems.at[16]))
    outs[-1].start()
    for out in outs:
        out.wait()


def per_device(query_in, key_in, value_in, short_taps, long_filter, cotangent):
    rows, channels = query_in.shape[1:]
    hbm = pl.BlockSpec(memory_space=pltpu.HBM)
    shape = jax.ShapeDtypeStruct
    results = (
        shape((rows, channels), BF16),
        shape((rows, channels), BF16),
        shape((rows, channels), BF16),
        shape(short_taps.shape, F32),
        shape((rows, channels), F32),
    )
    constants, back = tables()
    constants = [jnp.asarray(t) for t in constants]
    operands = [query_in[0], key_in[0], value_in[0], cotangent[0], long_filter, short_taps, *constants]
    scratch = [pltpu.VMEM(v.shape, v.dtype) for v in operands] + [
        pltpu.VMEM((PARTS, GROUP, ROWS, POS), BF16),
        pltpu.VMEM((PARTS, GROUP, ROWS, POS), BF16),
        pltpu.VMEM((GROUP, CHAN, POS), BF16),
        pltpu.VMEM((NCTX, CHAN, POS), BF16),
        pltpu.VMEM((GROUP * HELD, POS), F32),
        pltpu.VMEM((NCTX * 8, POS), F32),
        pltpu.VMEM((2 * SEQ * PAIR * NCTX, 2 * POS), F32),
        pltpu.VMEM((CHAN * NCTX, 2 * POS), F32),
        pltpu.VMEM((SEQ * PAIR, 2, NCTX, POS), F32),
        pltpu.VMEM((GROUP * HELD, POS), F32),
        pltpu.VMEM((PARTS, GROUP, ROWS, POS), BF16),
        pltpu.VMEM((PARTS, NCTX, PAIR * POS), F32),
        pltpu.VMEM((PARTS, NCTX, PAIR * POS), F32),
        pltpu.VMEM((POS, POS), F32),
        pltpu.VMEM((1, POS), F32),
        pltpu.VMEM((1, POS), F32),
        pltpu.VMEM((GROUP, 2, POS), F32),
        pltpu.SemaphoreType.DMA((len(operands),)),
        pltpu.SemaphoreType.DMA((PARTS,)),
        pltpu.SemaphoreType.DMA((PARTS,)),
        pltpu.SemaphoreType.DMA,
        pltpu.SemaphoreType.DMA,
        pltpu.SemaphoreType.DMA((PARTS,)),
        pltpu.SemaphoreType.DMA((PARTS,)),
        pltpu.SemaphoreType.DMA((2, PARTS)),
        pltpu.SemaphoreType.DMA((4,)),
        pltpu.SemaphoreType.REGULAR((NZ,)),
    ]
    params = functools.partial(pltpu.CompilerParams, vmem_limit_bytes=63 * 1024 * 1024)
    held = pl.pallas_call(
        kernel,
        out_shape=(shape((PARTS, GROUP, ROWS, POS), BF16), shape((GROUP, 2, POS), F32)),
        in_specs=[hbm] * len(operands),
        out_specs=[hbm] * 2,
        scratch_shapes=scratch,
        compiler_params=params(collective_id=0, has_side_effects=True),
    )(*operands)
    inner = [*held, jnp.asarray(back)]
    grad_query, grad_key, grad_value, grad_taps, grad_filter = pl.pallas_call(
        finish,
        out_shape=results,
        in_specs=[hbm] * 3,
        out_specs=[hbm] * 5,
        scratch_shapes=[pltpu.VMEM(v.shape, v.dtype) for v in (*inner, *results)]
        + [pltpu.SemaphoreType.DMA((6,)), pltpu.SemaphoreType.DMA((17,))],
        compiler_params=params(),
    )(*inner)
    return (grad_query[None], grad_key[None], grad_value[None], grad_taps, grad_filter)


def solution(mesh):
    seq = P("dp", "ctx", None)
    return jax.shard_map(
        per_device,
        mesh=mesh,
        in_specs=(seq, seq, seq, P(), P("ctx", None), seq),
        out_specs=(seq, seq, seq, P(), P("ctx", None)),
        check_vma=False,
    )
```

```python
import functools
import math

import jax
import jax.numpy as jnp
import numpy as np
from jax import lax
from jax.experimental import pallas as pl
from jax.experimental.pallas import tpu as pltpu
from jax.sharding import PartitionSpec as P

MESH = pl.DeviceIdType.MESH
F32 = jnp.float32
BF16 = jnp.bfloat16

NZ, NPLANE, NCTX = 8, 16, 64
GROUP = NZ * NPLANE
CHAN = 4
SEQ = 2
POS = 128
PARTS = 4
PAIR = CHAN // PARTS
ROWS = 4 * PAIR
HELD = 8


def split_np(table):
    high = table.astype(jnp.bfloat16)
    low = (table - high.astype(np.float64)).astype(jnp.bfloat16)
    return high, low


@functools.cache
def tables():
    length = NCTX * POS
    a = np.arange(NCTX, dtype=np.float64)
    b = np.arange(POS, dtype=np.float64)
    outer = 2 * np.pi * np.outer(a, a + 0.25) / NCTX
    turn = 2 * np.pi * np.outer(a + 0.25, b) / length
    inner = 2 * np.pi * (np.outer(b, b) % POS) / POS
    first = np.concatenate([np.cos(outer.T), -np.sin(outer.T)], axis=0)
    high, low = split_np(first)
    first_cat = np.concatenate([high, low, high], axis=1)
    scale = 1.0 / (length * math.sqrt(length))
    last = np.concatenate([np.cos(outer), -np.sin(outer)], axis=1) * scale
    high, low = split_np(last)
    last_cat = np.concatenate([high, low, high], axis=1)
    c, s = np.cos(inner), np.sin(inner)
    forward = np.stack(split_np(np.block([[c, -s], [s, c]])))
    inverse = np.stack(split_np(np.block([[c, s], [-s, c]])))
    twiddle = np.stack([np.cos(turn), np.sin(turn)]).astype(np.float32)
    pick = np.zeros((PARTS, 32, 4, PAIR, 4, POS), np.float32)
    pick_one = np.zeros((32, 8, POS), np.float32)
    for g in range(32):
        for i in range(CHAN):
            pick_one[g, i, CHAN * g + i] = 1
            for f in range(4):
                pick[i // PAIR, g, f, i % PAIR, f, CHAN * g + i] = 1
    back = pick.copy()
    back[:, :, 3] = 0
    back[1:, :, 3] = pick[:-1, :, 3]
    back = np.concatenate([back.reshape(512, 512), pick[-1, :, 3].reshape(32, 512)]).astype(jnp.bfloat16)
    pick = pick.reshape(512, 512).astype(jnp.bfloat16)
    pick_one = pick_one.reshape(256, POS).astype(jnp.bfloat16)
    return (first_cat, last_cat, forward, inverse, twiddle, pick_one, pick), back


def split(x):
    high = x.astype(BF16)
    return high, (x - high.astype(F32)).astype(BF16)


def dot(a, b):
    return jnp.dot(a, b, preferred_element_type=F32)


def dot_nt(a, b):
    return lax.dot_general(a, b, (((1,), (1,)), ((), ())), preferred_element_type=F32)


def stack_split(x):
    high, low = split(x)
    return jnp.concatenate([high, high, low], axis=0)


def wide_dot(x, table):
    high, low = split(x)
    return dot(high, table[0]) + (dot(high, table[1]) + dot(low, table[0]))


def wrap(v, n):
    return jnp.where(v >= n, v - n, v)


def kernel(
    q_hbm, k_hbm, v_hbm, c_hbm, filt_hbm, taps_hbm, first_hbm, last_hbm, fwd_hbm, inv_hbm, tw_hbm, pick1_hbm, pick_hbm,
    rrecv, tap_recv,
    q_ref, k_ref, v_ref, c_ref, filt_ref, taps_ref, first_ref, last_ref, fwd_ref, inv_ref, tw_ref, pick1_ref, pick_ref,
    send_buf, recv_buf, fsend, frecv, raw, fraw, spec, hspec, keep, pack, rsend,
    sib_send, sib_recv, tap_rows, tap_own, tap_sib, tap_send,
    load_sems, send_sem, recv_sem, fsend_sem, frecv_sem, rsend_sem, rrecv_sem,
    sib_sems, tap_sems, plane_sem,
):
    dp, cx = lax.axis_index("dp"), lax.axis_index("ctx")
    zh, core = dp // 2, lax.rem(dp, 2)
    y, zl, x = cx // 16, lax.rem(cx // 4, 4), lax.rem(cx, 4)
    z = zh * 4 + zl
    me = zh * NCTX + cx

    def plane_of(k):
        return wrap(z + k, NZ)

    sibling = (zh * 2 + (1 - core), cx)

    barrier = pltpu.get_barrier_semaphore()

    def signal_to(device, sem):
        pl.semaphore_signal(sem, inc=1, device_id=device, device_id_type=MESH)

    xs = [wrap(x + dx, 4) for dx in range(4)]
    ys = [wrap(y + dy, 4) * 16 for dy in range(4)]
    zs = []
    for dz in range(NZ):
        zt = plane_of(dz)
        half = zt // 4
        zs.append((half * 2 + core, (zt - 4 * half) * 4, half * NCTX))

    def target(dx, dy, dz):
        dp_t, zrow, first = zs[dz]
        ctx = ys[dy] + zrow + xs[dx]
        return (dp_t, ctx), first + ctx

    others = [
        (dx, dy, dz)
        for dz in (4, 3, 5, 2, 6, 1, 7, 0) for dy in (2, 1, 3, 0) for dx in (2, 1, 3, 0) if dx or dy or dz
    ]
    for d in others:
        signal_to(target(*d)[0], barrier)
    signal_to(sibling, barrier)

    loads = [
        pltpu.make_async_copy(source, target, load_sems.at[n])
        for n, (source, target) in enumerate([
            (pick_hbm, pick_ref), (q_hbm, q_ref), (k_hbm, k_ref), (v_hbm, v_ref), (c_hbm, c_ref),
            (filt_hbm, filt_ref), (pick1_hbm, pick1_ref), (first_hbm, first_ref), (fwd_hbm, fwd_ref), (tw_hbm, tw_ref),
            (taps_hbm, taps_ref), (inv_hbm, inv_ref), (last_hbm, last_ref),
        ])
    ]
    for load in loads:
        load.start()
    for load in loads[:5]:
        load.wait()

    for j in range(4):
        lanes = slice(j * POS, (j + 1) * POS)
        fields = jnp.concatenate([q_ref[:, lanes], k_ref[:, lanes], v_ref[:, lanes], c_ref[:, lanes]], axis=1)
        rows = dot_nt(pick_ref[...], fields).astype(BF16)
        send_buf[:, pl.ds(j * 32, 32)] = rows.reshape(PARTS, 32, ROWS, POS)
    loads[5].wait()
    loads[6].wait()
    for j in range(4):
        lanes = slice(j * POS, (j + 1) * POS)
        rows = dot_nt(pick1_ref[...], filt_ref[:, lanes].astype(BF16))
        fsend[pl.ds(j * 32, 32)] = rows.reshape(32, 8, POS)[:, :CHAN, :].astype(BF16)

    for part in range(PARTS):
        pltpu.make_async_copy(send_buf.at[part, me], recv_buf.at[part, me], recv_sem.at[part]).start()
    fown = pltpu.make_async_copy(fsend.at[me], frecv.at[cx], frecv_sem)
    fown.start()

    pl.semaphore_wait(barrier, GROUP)
    near = (0, 1, 2, 7)
    others = [
        (dx, dy, dz)
        for dy in (2, 1, 3, 0) for dx in (2, 1, 3, 0) for dz in (4, 3, 5, 2, 6, 1, 7, 0) if dx or dy or dz
    ]
    for part in range(PARTS):
        for d in others:
            to, owner = target(*d)
            pltpu.make_async_remote_copy(
                src_ref=send_buf.at[part, owner], dst_ref=recv_buf.at[part, me],
                send_sem=send_sem.at[part], recv_sem=recv_sem.at[part], device_id=to, device_id_type=MESH,
            ).start()
            if part == 0 and d[2] in near:
                pltpu.make_async_remote_copy(
                    src_ref=fsend.at[owner], dst_ref=frecv.at[cx], send_sem=fsend_sem, recv_sem=frecv_sem,
                    device_id=to, device_id_type=MESH,
                ).start()

    def wait_bytes(ref, sem):
        pltpu.make_async_copy(ref, ref, sem).wait()

    row_id = lax.broadcasted_iota(jnp.int32, (NCTX, POS), 0)
    lane_id = lax.broadcasted_iota(jnp.int32, (NCTX, POS), 1)

    def before(v, s):
        turned = pltpu.roll(v, s, 1)
        carried = jnp.where(row_id == 0, 0.0, pltpu.roll(turned, 1, 0))
        return jnp.where(lane_id < s, carried, turned)

    def after(v, s):
        turned = pltpu.roll(v, POS - s, 1)
        carried = jnp.where(row_id == NCTX - 1, 0.0, pltpu.roll(turned, NCTX - 1, 0))
        return jnp.where(lane_id >= POS - s, carried, turned)

    for load in loads[7:]:
        load.wait()
    channel = lax.broadcasted_iota(jnp.int32, (3, GROUP * CHAN), 1)
    tap_values = [
        [jnp.sum(jnp.where(channel == me * CHAN + i, taps_ref[branch], 0.0), axis=1, keepdims=True) for i in range(CHAN)]
        for branch in range(3)
    ]

    def tap(branch, j, i):
        return tap_values[branch][i][j:j + 1]

    def field(h, f, i):
        return raw[pl.ds(h * NCTX * HELD + f * PAIR + i, NCTX, HELD), :]

    cos, sin = tw_ref[0], tw_ref[1]

    def spectrum(values):
        turned = dot(first_ref[...], stack_split(jnp.concatenate(values, axis=1)))
        parts = []
        for n in range(len(values)):
            re, im = turned[:NCTX, n * POS:(n + 1) * POS], turned[NCTX:, n * POS:(n + 1) * POS]
            parts.append(jnp.concatenate([re * cos + im * sin, im * cos - re * sin], axis=1))
        return wide_dot(jnp.concatenate(parts, axis=0), fwd_ref)

    def signal(spectra):
        joined = jnp.concatenate([jnp.concatenate(s, axis=1) for s in spectra], axis=0)
        turned = wide_dot(joined, inv_ref)
        parts = []
        for n in range(len(spectra)):
            re, im = turned[n * NCTX:(n + 1) * NCTX, :POS], turned[n * NCTX:(n + 1) * NCTX, POS:]
            parts.append(jnp.concatenate([re * cos - im * sin, re * sin + im * cos], axis=0))
        return dot(last_ref[...], stack_split(jnp.concatenate(parts, axis=1)))

    def halves(ref, n):
        return ref[n * NCTX:(n + 1) * NCTX, :POS], ref[n * NCTX:(n + 1) * NCTX, POS:]

    wait_bytes(frecv, frecv_sem)
    filt = frecv[...].astype(F32)
    fraw[...] = jnp.concatenate([filt, jnp.zeros_like(filt)], axis=1).reshape(NCTX * 8, POS)
    hspec[...] = spectrum([fraw[pl.ds(i, NCTX, 8), :] for i in range(CHAN)])

    tap_rows[...] = jnp.zeros_like(tap_rows)
    pairs = [(h, i) for h in range(SEQ) for i in range(PAIR)]
    sibs = []

    def filter_total(part):
        sibs[part].wait()
        return sib_send[part] + sib_recv[part]

    def filter_rows(part):
        total = filter_total(part)
        for h in range(SEQ):
            pack[pl.ds(h * NCTX * HELD + 3, NCTX, HELD), :] = total

    pack[...] = jnp.zeros_like(pack)
    for part in range(PARTS):
        wait_bytes(recv_buf.at[part], recv_sem.at[part])
        arrived = recv_buf[part].astype(F32)
        raw[...] = jnp.concatenate([arrived, jnp.zeros_like(arrived)], axis=1).reshape(GROUP * HELD, POS)
        values, delayed = [], []
        for n, (h, i) in enumerate(pairs):
            feats = []
            for branch in range(3):
                v = field(h, branch, i)
                c = part * PAIR + i
                delayed.append((v, before(v, 1), before(v, 2)))
                feats.append(sum(tap(branch, j, c) * delayed[-1][j] for j in range(3)))
            keep[n, 0] = feats[1]
            keep[n, 1] = feats[2]
            values += [feats[1] * feats[2], feats[0] * field(h, 3, i)]
        spec[...] = spectrum(values)

        corrs = []
        for i in range(PAIR):
            re = im = 0.0
            for h in range(SEQ):
                n = h * PAIR + i
                mr, mi = halves(spec, 2 * n)
                gr, gi = halves(spec, 2 * n + 1)
                re, im = re + (mr * gr + mi * gi), im + (mr * gi - mi * gr)
            corrs.append((re, im))
        sib_send[part] = signal(corrs)
        sib = pltpu.make_async_remote_copy(
            src_ref=sib_send.at[part], dst_ref=sib_recv.at[part],
            send_sem=sib_sems.at[0, part], recv_sem=sib_sems.at[1, part], device_id=sibling, device_id_type=MESH,
        )
        sib.start()
        sibs.append(sib)

        spectra = []
        for n, (h, i) in enumerate(pairs):
            fr, fi = halves(hspec, part * PAIR + i)
            mr, mi = halves(spec, 2 * n)
            gr, gi = halves(spec, 2 * n + 1)
            spectra += [(fr * mr - fi * mi, fr * mi + fi * mr), (fr * gr + fi * gi, fr * gi - fi * gr)]
        back = signal(spectra)
        grads = []
        for n, (h, i) in enumerate(pairs):
            conv = back[:, 2 * n * POS:(2 * n + 1) * POS]
            adj = back[:, (2 * n + 1) * POS:(2 * n + 2) * POS]
            grads.append([field(h, 3, i) * conv, adj * keep[n, 1], adj * keep[n, 0]])
            c = part * PAIR + i
            for branch in range(3):
                d = grads[n][branch]
                pack[pl.ds(h * NCTX * HELD + branch * PAIR + i, NCTX, HELD), :] = (
                    tap(branch, 0, c) * d + tap(branch, 1, c) * after(d, 1) + tap(branch, 2, c) * after(d, 2)
                )

        def tap_terms():
            for n, (h, i) in enumerate(pairs):
                for branch in range(3):
                    d = grads[n][branch]
                    for j in range(3):
                        term = d * delayed[n * 3 + branch][j]
                        row = (branch * 3 + j) * CHAN + part * PAIR + i
                        tap_rows[row:row + 1, :] += jnp.sum(term, axis=0, keepdims=True)

        def give():
            if part:
                filter_rows(part - 1)
            rsend[part] = pack[...].reshape(GROUP, HELD, POS)[:, :ROWS, :].astype(BF16)
            for d in others:
                to, owner = target(*d)
                pltpu.make_async_remote_copy(
                    src_ref=rsend.at[part, owner], dst_ref=rrecv.at[part, me],
                    send_sem=rsend_sem.at[part], recv_sem=rrecv_sem.at[part], device_id=to, device_id_type=MESH,
                ).start()
            pltpu.make_async_copy(rsend.at[part, me], rrecv.at[part, me], rrecv_sem.at[part]).start()

        if part < PARTS - 1:
            give()
            tap_terms()
        else:
            tap_terms()
            ones = jnp.ones((8, POS), BF16)
            scale = 1.0 / math.sqrt(SEQ * 2 * NCTX * POS)
            high, low = split(tap_rows[...])
            tap_own[...] = (dot_nt(ones, high) + dot_nt(ones, low))[0:1] * scale
            tap_sibling = pltpu.make_async_remote_copy(
                src_ref=tap_own, dst_ref=tap_sib, send_sem=tap_sems.at[0], recv_sem=tap_sems.at[1],
                device_id=sibling, device_id_type=MESH,
            )
            tap_sibling.start()
            give()
    tap_sibling.wait()
    total = filter_total(PARTS - 1).reshape(NCTX, 1, POS)
    for h in range(SEQ):
        tap_send[pl.ds(h * NCTX, NCTX), 0:1, :] = total
    tap_send[:, 1:2, :] = jnp.broadcast_to((tap_own[...] + tap_sib[...]).reshape(1, 1, POS), (GROUP, 1, POS))
    for d in others:
        to, owner = target(*d)
        pltpu.make_async_remote_copy(
            src_ref=tap_send.at[owner], dst_ref=tap_recv.at[me], send_sem=tap_sems.at[2], recv_sem=tap_sems.at[3],
            device_id=to, device_id_type=MESH,
        ).start()
    pltpu.make_async_copy(tap_send.at[me], tap_recv.at[me], tap_sems.at[3]).start()

    wait_bytes(fsend.at[pl.ds(0, NCTX - 1)], fsend_sem)
    for part in range(PARTS):
        wait_bytes(send_buf.at[part, pl.ds(0, GROUP - 1)], send_sem.at[part])
    for part in range(PARTS):
        wait_bytes(rsend.at[part, pl.ds(0, GROUP - 1)], rsend_sem.at[part])
    wait_bytes(tap_recv.at[pl.ds(0, GROUP - 1)], tap_sems.at[2])
    for part in range(PARTS):
        wait_bytes(rrecv.at[part], rrecv_sem.at[part])
    wait_bytes(tap_recv, tap_sems.at[3])


def finish(
    rows_hbm, taps_hbm, pick_hbm, gq_hbm, gk_hbm, gv_hbm, gt_hbm, gf_hbm,
    rows_ref, taps_ref, pick_ref, gq_ref, gk_ref, gv_ref, gt_ref, gf_ref, load_sems, out_sems,
):
    load_pick = pltpu.make_async_copy(pick_hbm, pick_ref, load_sems.at[0])
    load_pick.start()
    loads = [
        pltpu.make_async_copy(rows_hbm.at[:, pl.ds(j * 32, 32)], rows_ref.at[:, pl.ds(j * 32, 32)], load_sems.at[1 + j])
        for j in range(4)
    ]
    for load in loads:
        load.start()
    load_taps = pltpu.make_async_copy(taps_hbm, taps_ref, load_sems.at[5])
    load_taps.start()
    row = lax.broadcasted_iota(jnp.int32, (CHAN * 16, POS), 0)
    lane = lax.broadcasted_iota(jnp.int32, (CHAN * 16, POS), 1)
    pick_row = (lane == CHAN * (row % 16) + row // 16).astype(F32).astype(BF16)
    row = lax.broadcasted_iota(jnp.int32, (CHAN * GROUP, GROUP * CHAN), 0)
    lane = lax.broadcasted_iota(jnp.int32, (CHAN * GROUP, GROUP * CHAN), 1)
    spread = (lane == CHAN * (row % GROUP) + row // GROUP).astype(F32).astype(BF16)
    load_pick.wait()
    load_taps.wait()
    outs = []
    for j in range(4):
        lanes = pl.ds(j * POS, POS)
        loads[j].wait()
        rows = jnp.concatenate([
            rows_ref[:, pl.ds(j * 32, 32)].reshape(512, POS),
            taps_ref[pl.ds(j * 32, 32), 0, :].astype(BF16),
        ], axis=0)
        out = lax.dot_general(rows, pick_ref[...], (((0,), (0,)), ((), ())), preferred_element_type=F32)
        gq_ref[:, lanes] = out[:, :POS].astype(BF16)
        gk_ref[:, lanes] = out[:, POS:2 * POS].astype(BF16)
        gv_ref[:, lanes] = out[:, 2 * POS:3 * POS].astype(BF16)
        gf_ref[:, lanes] = out[:, 3 * POS:]
        for n, (source, target) in enumerate([(gq_ref, gq_hbm), (gk_ref, gk_hbm), (gv_ref, gv_hbm), (gf_ref, gf_hbm)]):
            outs.append(pltpu.make_async_copy(source.at[:, lanes], target.at[:, lanes], out_sems.at[4 * j + n]))
            outs[-1].start()

    high, low = split(taps_ref[:, 1, :])
    rows = dot_nt(pick_row, high) + dot_nt(pick_row, low)
    high, low = split(jnp.concatenate([rows[i * 16:(i + 1) * 16] for i in range(CHAN)], axis=1))
    both = dot(jnp.concatenate([high, low], axis=0), spread)
    total = both[:16] + both[16:]
    for branch in range(3):
        gt_ref[branch] = total[branch * 3:branch * 3 + 3]
    outs.append(pltpu.make_async_copy(gt_ref, gt_hbm, out_sems.at[16]))
    outs[-1].start()
    for out in outs:
        out.wait()


def per_device(query_in, key_in, value_in, short_taps, long_filter, cotangent):
    rows, channels = query_in.shape[1:]
    hbm = pl.BlockSpec(memory_space=pltpu.HBM)
    shape = jax.ShapeDtypeStruct
    results = (
        shape((rows, channels), BF16),
        shape((rows, channels), BF16),
        shape((rows, channels), BF16),
        shape(short_taps.shape, F32),
        shape((rows, channels), F32),
    )
    constants, back = tables()
    constants = [jnp.asarray(t) for t in constants]
    operands = [query_in[0], key_in[0], value_in[0], cotangent[0], long_filter, short_taps, *constants]
    scratch = [pltpu.VMEM(v.shape, v.dtype) for v in operands] + [
        pltpu.VMEM((PARTS, GROUP, ROWS, POS), BF16),
        pltpu.VMEM((PARTS, GROUP, ROWS, POS), BF16),
        pltpu.VMEM((GROUP, CHAN, POS), BF16),
        pltpu.VMEM((NCTX, CHAN, POS), BF16),
        pltpu.VMEM((GROUP * HELD, POS), F32),
        pltpu.VMEM((NCTX * 8, POS), F32),
        pltpu.VMEM((2 * SEQ * PAIR * NCTX, 2 * POS), F32),
        pltpu.VMEM((CHAN * NCTX, 2 * POS), F32),
        pltpu.VMEM((SEQ * PAIR, 2, NCTX, POS), F32),
        pltpu.VMEM((GROUP * HELD, POS), F32),
        pltpu.VMEM((PARTS, GROUP, ROWS, POS), BF16),
        pltpu.VMEM((PARTS, NCTX, PAIR * POS), F32),
        pltpu.VMEM((PARTS, NCTX, PAIR * POS), F32),
        pltpu.VMEM((POS, POS), F32),
        pltpu.VMEM((1, POS), F32),
        pltpu.VMEM((1, POS), F32),
        pltpu.VMEM((GROUP, 2, POS), F32),
        pltpu.SemaphoreType.DMA((len(operands),)),
        pltpu.SemaphoreType.DMA((PARTS,)),
        pltpu.SemaphoreType.DMA((PARTS,)),
        pltpu.SemaphoreType.DMA,
        pltpu.SemaphoreType.DMA,
        pltpu.SemaphoreType.DMA((PARTS,)),
        pltpu.SemaphoreType.DMA((PARTS,)),
        pltpu.SemaphoreType.DMA((2, PARTS)),
        pltpu.SemaphoreType.DMA((4,)),
        pltpu.SemaphoreType.REGULAR((NZ,)),
    ]
    params = functools.partial(pltpu.CompilerParams, vmem_limit_bytes=63 * 1024 * 1024)
    held = pl.pallas_call(
        kernel,
        out_shape=(shape((PARTS, GROUP, ROWS, POS), BF16), shape((GROUP, 2, POS), F32)),
        in_specs=[hbm] * len(operands),
        out_specs=[hbm] * 2,
        scratch_shapes=scratch,
        compiler_params=params(collective_id=0, has_side_effects=True),
    )(*operands)
    inner = [*held, jnp.asarray(back)]
    grad_query, grad_key, grad_value, grad_taps, grad_filter = pl.pallas_call(
        finish,
        out_shape=results,
        in_specs=[hbm] * 3,
        out_specs=[hbm] * 5,
        scratch_shapes=[pltpu.VMEM(v.shape, v.dtype) for v in (*inner, *results)]
        + [pltpu.SemaphoreType.DMA((6,)), pltpu.SemaphoreType.DMA((17,))],
        compiler_params=params(),
    )(*inner)
    return (grad_query[None], grad_key[None], grad_value[None], grad_taps, grad_filter)


def solution(mesh):
    seq = P("dp", "ctx", None)
    return jax.shard_map(
        per_device,
        mesh=mesh,
        in_specs=(seq, seq, seq, P(), P("ctx", None), seq),
        out_specs=(seq, seq, seq, P(), P("ctx", None)),
        check_vma=False,
    )
```
